32 devices in a mesh: dp: 4 (over z), seq: 8 (over y, x, core).
Axes of the slice: x: 2, y: 2, z: 4, core: 2. Of those that a mesh axis runs over, the one named last changes fastest.
Arguments:
- tokens: bfloat16 [4096, 2688], P(('dp', 'seq')), may hold values from -6 to 6
- q_weight: bfloat16 [2688, 4096], P('dp', 'seq'), may hold values from -0.125 to 0.125
- key_projection: bfloat16 [2688, 2048], P('dp', 'seq'), may hold values from -0.125 to 0.125
- value_projection: bfloat16 [2688, 2048], P('dp', 'seq'), may hold values from -0.125 to 0.125
- query_norm_gain: float32 [128], replicated, may hold values from 0.5 to 2.5
- key_norm_gain: float32 [128], replicated, may hold values from 0.5 to 2.5
- doc_lengths: int32 [4, 4], P('dp'), may hold values from 1 to 768, 1024 in all within a row
- out_cot: bfloat16 [4096, 4096], P('dp', 'seq'), may hold values from -6 to 6
Outputs:
- attn_out: bfloat16 [4096, 4096], P(('dp', 'seq'))
- token_grad: bfloat16 [4096, 2688], P(('dp', 'seq'))
- q_weight_grad: float32 [2688, 4096], P('dp', 'seq')
- k_weight_grad: float32 [2688, 2048], P('dp', 'seq')
- v_weight_grad: float32 [2688, 2048], P('dp', 'seq')
The draws below stay inside these ranges and needn't reach their ends.
Inputs may be any that keep to these rules, and one draw needn't show every extreme that they name: `doc_lengths`: each row's 4 lengths add up to 1024, and in every row the longest document has exactly 768 tokens.
All inputs are finite; a program needn't handle non-finite values.
Results may differ from the reference program's by a relative error of at most 0.015.
Values may be sent and summed in bfloat16 or wider, within the bound.
No kernel may reach another device: no remote copies, remote signals or barrier semaphores. Data moves between devices by JAX's collectives and lax.ppermute only.
A program may use at most 128 MiB of HBM per device.

```python
import math
import jax
import jax.numpy as jnp
import numpy as np
from jax import lax

MODEL_WIDTH = 2688
QUERY_HEADS = 32
KEY_VALUE_HEADS = 16
HEAD_WIDTH = 128
WINDOW = 1024
DOCS = 4
SEQ_LEN = 1024
ROWS = 4096
HQ_DEV = 4
KV_DEV = 2
N_DP = 4


def steps_of(rng, extent, split, low, high):
    def one(dim, parts):
        steps = jax.random.uniform(jax.random.fold_in(jax.random.fold_in(rng, 6), dim), (parts,), jnp.float32, low / len(split), high / len(split))
        return jnp.repeat(jnp.exp(steps), extent[dim] // parts).reshape((-1,) + (1,) * (len(extent) - dim - 1))

    level = one(*split[0])
    for cut in split[1:]:
        level = level * one(*cut)
    return level


def split_up(amount, total, most, skew):
    weights = [(1 << 20) // math.isqrt(rank ** skew) + 1 for rank in range(2, amount + 1)]
    surplus, counts = total - most - (amount - 1), [1] * (amount - 1)
    while surplus > 0:
        movable = [i for i in range(amount - 1) if counts[i] < most]
        whole, budget = sum([weights[i] for i in movable]), surplus
        for i in movable:
            addition = min(most - counts[i], max(1, budget * weights[i] // whole), surplus)
            counts[i] = counts[i] + addition
            surplus = surplus - addition
    return np.array([most] + counts)


def ragged_sizes(rng, number_of, total, bound, lean):
    if number_of == 2:
        one = jax.random.randint(rng, (), max(1, total - bound), min(bound, total - 1) + 1)
        return jnp.stack([one, total - one])
    tallies = jnp.asarray(split_up(number_of, total, bound, lean), jnp.int32)
    twos = (number_of - 1) // 2
    source_of, receiver = tallies[1:1 + 2 * twos:2], tallies[2:2 + 2 * twos:2]
    room = jnp.minimum(source_of - 1, bound - receiver)
    shifted = jax.random.randint(jax.random.fold_in(rng, 1), (twos,), 0, 1 << 20) % (room + 1)
    tallies = tallies.at[1:1 + 2 * twos:2].set(source_of - shifted).at[2:2 + 2 * twos:2].set(receiver + shifted)
    return tallies[jax.random.permutation(jax.random.fold_in(rng, 2), number_of)]


def normal_values(key, dims, scale, bound, cuts=(), kind=jnp.bfloat16):
    values = scale * jax.random.normal(key, dims, jnp.float32)
    if cuts:
        values = values * steps_of(key, dims, cuts, -0.22, 0.18)
    return jnp.clip(values, -bound, bound).astype(kind)


def setup_inputs(seed: int = 0) -> dict:
    key_list = jax.random.split(jax.random.key(seed), 9)
    tokens = normal_values(key_list[0], (ROWS, MODEL_WIDTH), 1.0, 6.0, ((0, 32),))
    q_weight = normal_values(key_list[1], (MODEL_WIDTH, QUERY_HEADS * HEAD_WIDTH), MODEL_WIDTH ** -0.5, 0.125, ((0, 4), (1, 8)))
    key_projection = normal_values(key_list[2], (MODEL_WIDTH, KEY_VALUE_HEADS * HEAD_WIDTH), MODEL_WIDTH ** -0.5, 0.125, ((0, 4), (1, 8)))
    value_projection = normal_values(key_list[3], (MODEL_WIDTH, KEY_VALUE_HEADS * HEAD_WIDTH), MODEL_WIDTH ** -0.5, 0.125, ((0, 4), (1, 8)))
    query_norm_gain = jnp.clip(jnp.exp(jax.random.uniform(key_list[4], (HEAD_WIDTH,), jnp.float32, math.log(0.5), math.log(2.5))), 0.5, 2.5)
    key_norm_gain = jnp.clip(jnp.exp(jax.random.uniform(key_list[5], (HEAD_WIDTH,), jnp.float32, math.log(0.5), math.log(2.5))), 0.5, 2.5)
    doc_lengths = jax.vmap(lambda own: ragged_sizes(own, DOCS, SEQ_LEN, 3 * SEQ_LEN // 4, 1))(jax.random.split(key_list[6], N_DP)).reshape((N_DP, DOCS)).astype(jnp.int32)
    out_cot = normal_values(key_list[7], (ROWS, QUERY_HEADS * HEAD_WIDTH), 1.0, 6.0, ((0, 4), (1, 8)))
    return {"tokens": tokens, "q_weight": q_weight, "key_projection": key_projection, "value_projection": value_projection, "query_norm_gain": query_norm_gain, "key_norm_gain": key_norm_gain, "doc_lengths": doc_lengths, "out_cot": out_cot}


score_scale = 168.0 ** (-0.5)
rope_base = 10000.0
norm_eps = 1e-06

def doc_layout(length_row, length):
    ends = jnp.cumsum(length_row, dtype=jnp.int32)
    starts = ends - length_row
    token = jnp.arange(length, dtype=jnp.int32)
    doc_index = lax.optimization_barrier(jnp.sum((token[:, None] >= ends[None, :]).astype(jnp.int32), axis=1, dtype=jnp.int32))
    member = doc_index[:, None] == jnp.arange(length_row.shape[0], dtype=jnp.int32)[None, :]
    position = token - lax.optimization_barrier(jnp.sum(jnp.where(member, starts[None, :], 0), axis=1, dtype=jnp.int32))
    return (doc_index, position)

def rope_tables(position, head_size):
    half = head_size // 2
    inverse = rope_base ** (-jnp.arange(half, dtype=jnp.float32) * (2.0 / head_size))
    angle = position.astype(jnp.float32)[:, None] * inverse[None, :]
    cosine = jnp.concatenate([jnp.cos(angle), jnp.cos(angle)], axis=1)
    sine = jnp.concatenate([jnp.sin(angle), jnp.sin(angle)], axis=1)
    return (cosine, sine)

def norm_rotate(vectors, gain, cosine, sine):
    factor = lax.rsqrt(lax.optimization_barrier(jnp.mean(vectors * vectors, axis=-1, keepdims=True)) + norm_eps)
    normed = vectors * factor * gain
    half = vectors.shape[-1] // 2
    turned = jnp.concatenate([-normed[..., half:], normed[..., :half]], axis=-1)
    return normed * cosine[:, None, :] + turned * sine[:, None, :]

def shape_heads(projected_rows, query_norm_gain, key_norm_gain, cosine, sine, query_heads, value_heads, head_size):
    length = projected_rows.shape[0]
    query_cols = query_heads * head_size
    key_columns = value_heads * head_size
    queries = projected_rows[:, :query_cols].reshape(length, query_heads, head_size)
    keys = projected_rows[:, query_cols:query_cols + key_columns].reshape(length, value_heads, head_size)
    values = projected_rows[:, query_cols + key_columns:].reshape(length, value_heads, head_size)
    return (norm_rotate(queries, query_norm_gain, cosine, sine), norm_rotate(keys, key_norm_gain, cosine, sine), values)

def band_mask(doc_index, query_start, key_start, query_rows, key_rows):
    query_pos = query_start + jnp.arange(query_rows, dtype=jnp.int32)
    key_pos = key_start + jnp.arange(key_rows, dtype=jnp.int32)
    query_doc = lax.dynamic_slice_in_dim(doc_index, query_start, query_rows, 0)
    key_doc = lax.dynamic_slice_in_dim(doc_index, key_start, key_rows, 0)
    spacing = query_pos[:, None] - key_pos[None, :]
    return (query_doc[:, None] == key_doc[None, :]) & (spacing >= 0) & (spacing < WINDOW)

def block_probs(query_part, key_part, allowed):
    scores = jnp.einsum('qhgd,khd->hgqk', query_part, key_part, preferred_element_type=jnp.float32) * score_scale
    weights = jnp.where(allowed[None, None], jnp.exp(scores), 0.0)
    return weights / lax.optimization_barrier(jnp.sum(weights, axis=-1, keepdims=True))

def layer_kernel(projected_rows, length_row, cotangent, query_norm_gain, key_norm_gain, query_heads, value_heads):
    length = projected_rows.shape[0]
    doc_index, position = doc_layout(length_row, length)
    cosine, sine = rope_tables(position, HEAD_WIDTH)
    (queries, keys, values), pull = jax.vjp(lambda inner: shape_heads(inner, query_norm_gain, key_norm_gain, cosine, sine, query_heads, value_heads, HEAD_WIDTH), projected_rows)
    group = query_heads // value_heads
    query_bf = queries.astype(jnp.bfloat16).reshape(length, value_heads, group, HEAD_WIDTH)
    key_bf = keys.astype(jnp.bfloat16)
    value_bf = values.astype(jnp.bfloat16)
    grad_out = cotangent.reshape(length, value_heads, group, HEAD_WIDTH)
    query_rows = min(512, length)
    key_rows = min(length, query_rows + WINDOW)
    blocks = length // query_rows

    def block_view(index):
        index = index.astype(jnp.int32)
        query_start = index * query_rows
        key_start = jnp.maximum(query_start + query_rows - key_rows, 0)
        query_part = lax.dynamic_slice_in_dim(query_bf, query_start, query_rows, 0)
        key_part = lax.dynamic_slice_in_dim(key_bf, key_start, key_rows, 0)
        value_part = lax.dynamic_slice_in_dim(value_bf, key_start, key_rows, 0)
        allowed = band_mask(doc_index, query_start, key_start, query_rows, key_rows)
        return (query_start, key_start, query_part, key_part, value_part, block_probs(query_part, key_part, allowed))

    def forward_block(index):
        _, _, _, _, value_part, probs = block_view(index)
        mixed = jnp.einsum('hgqk,khd->qhgd', probs.astype(jnp.bfloat16), value_part, preferred_element_type=jnp.float32)
        return mixed.astype(jnp.bfloat16).reshape(query_rows, query_heads * HEAD_WIDTH)
    head_output = lax.map(forward_block, jnp.arange(blocks, dtype=jnp.int32)).reshape(length, query_heads * HEAD_WIDTH)

    def backward_block(index, carry):
        grad_query, grad_key, grad_value = carry
        query_start, key_start, query_part, key_part, value_part, probs = block_view(index)
        grad_part = lax.dynamic_slice_in_dim(grad_out, query_start, query_rows, 0)
        probs_bf = probs.astype(jnp.bfloat16)
        value_term = jnp.einsum('hgqk,qhgd->khd', probs_bf, grad_part, preferred_element_type=jnp.float32)
        grad_probs = jnp.einsum('qhgd,khd->hgqk', grad_part, value_part, preferred_element_type=jnp.float32)
        delta = lax.optimization_barrier(jnp.sum(probs * grad_probs, axis=-1, keepdims=True))
        grad_scores = (probs * (grad_probs - delta)).astype(jnp.bfloat16)
        query_term = jnp.einsum('hgqk,khd->qhgd', grad_scores, key_part, preferred_element_type=jnp.float32) * score_scale
        key_term = jnp.einsum('hgqk,qhgd->khd', grad_scores, query_part, preferred_element_type=jnp.float32) * score_scale
        grad_query = lax.dynamic_update_slice_in_dim(grad_query, query_term, query_start, 0)
        grad_key = lax.dynamic_update_slice_in_dim(grad_key, lax.dynamic_slice_in_dim(grad_key, key_start, key_rows, 0) + key_term, key_start, 0)
        grad_value = lax.dynamic_update_slice_in_dim(grad_value, lax.dynamic_slice_in_dim(grad_value, key_start, key_rows, 0) + value_term, key_start, 0)
        return (grad_query, grad_key, grad_value)
    start_grads = (jnp.zeros((length, value_heads, group, HEAD_WIDTH), jnp.float32), jnp.zeros((length, value_heads, HEAD_WIDTH), jnp.float32), jnp.zeros((length, value_heads, HEAD_WIDTH), jnp.float32))
    grad_query, grad_key, grad_value = lax.fori_loop(0, blocks, backward_block, start_grads)
    projection_gradient, = pull((grad_query.reshape(length, query_heads, HEAD_WIDTH), grad_key, grad_value))
    return (head_output, projection_gradient.astype(jnp.bfloat16))

def reference(tokens, q_weight, key_projection, value_projection, query_norm_gain, key_norm_gain, doc_lengths, out_cot):
    joined = jnp.concatenate([q_weight, key_projection, value_projection], axis=1)
    query_cols = QUERY_HEADS * HEAD_WIDTH
    key_columns = KEY_VALUE_HEADS * HEAD_WIDTH

    def one_row(grads, row):
        row = row.astype(jnp.int32)
        first = row * SEQ_LEN
        row_tokens = lax.dynamic_slice_in_dim(tokens, first, SEQ_LEN, 0)
        row_cotangent = lax.dynamic_slice_in_dim(out_cot, first, SEQ_LEN, 0)
        length_row = lax.dynamic_index_in_dim(doc_lengths, row, 0, keepdims=False)
        projected_rows = jnp.dot(row_tokens, joined, preferred_element_type=jnp.float32)
        head_output, projection_gradient = layer_kernel(projected_rows, length_row, row_cotangent, query_norm_gain, key_norm_gain, QUERY_HEADS, KEY_VALUE_HEADS)

        def add_group(index, summed):
            index = index.astype(jnp.int32)
            pieces = []
            weights = []
            for base, width in ((0, HQ_DEV * HEAD_WIDTH), (query_cols, KV_DEV * HEAD_WIDTH), (query_cols + key_columns, KV_DEV * HEAD_WIDTH)):
                first_col = base + index * width
                pieces.append(lax.dynamic_slice_in_dim(projection_gradient, first_col, width, 1))
                weights.append(lax.dynamic_slice_in_dim(joined, first_col, width, 1))
            group_grad = jnp.concatenate(pieces, axis=1)
            group_weight = jnp.concatenate(weights, axis=1)
            term = lax.dot_general(group_grad, group_weight, (((1,), (1,)), ((), ())), preferred_element_type=jnp.float32)
            rounded = lax.optimization_barrier(term.astype(jnp.bfloat16))
            return summed + rounded.astype(jnp.float32)
        token_grad = lax.fori_loop(0, QUERY_HEADS // HQ_DEV, add_group, jnp.zeros((SEQ_LEN, MODEL_WIDTH), jnp.float32)).astype(jnp.bfloat16)
        grads = grads + lax.dot_general(row_tokens, projection_gradient, (((0,), (0,)), ((), ())), preferred_element_type=jnp.float32)
        return (grads, (head_output, token_grad))
    start_grads = jnp.zeros((MODEL_WIDTH, query_cols + 2 * key_columns), jnp.float32)
    grads, (outs, token_grads) = lax.scan(one_row, start_grads, jnp.arange(N_DP, dtype=jnp.int32))
    attn_out = outs.reshape(N_DP * SEQ_LEN, query_cols)
    token_grad = token_grads.reshape(N_DP * SEQ_LEN, MODEL_WIDTH)
    return (attn_out, token_grad, grads[:, :query_cols], grads[:, query_cols:query_cols + key_columns], grads[:, query_cols + key_columns:])
```

```python
import functools

import jax
import jax.numpy as jnp
from jax import lax
from jax.experimental import pallas as pl
from jax.experimental.pallas import tpu as pltpu
from jax.sharding import PartitionSpec as P

HEAD_WIDTH = 128
WINDOW = 1024
QUERY_BLOCK = 256

score_scale = 168.0 ** (-0.5)
rope_base = 10000.0
norm_eps = 1e-06
NN = (((1,), (0,)), ((), ()))
NT = (((1,), (1,)), ((), ()))
TN = (((0,), (0,)), ((), ()))


def dot(a, b, dims):
    return lax.dot_general(a, b, dims, preferred_element_type=jnp.float32)


def doc_tables(length_row, length):
    ends = jnp.cumsum(length_row, dtype=jnp.int32)
    starts = ends - length_row
    token = jnp.arange(length, dtype=jnp.int32)
    inside = (token[:, None] >= starts[None, :]) & (token[:, None] < ends[None, :])
    start = jnp.sum(jnp.where(inside, starts[None, :], 0), axis=1, dtype=jnp.int32)
    half = HEAD_WIDTH // 2
    inverse = rope_base ** (-jnp.arange(half, dtype=jnp.float32) * (2.0 / HEAD_WIDTH))
    angle = (token - start).astype(jnp.float32)[:, None] * inverse[None, :]
    cosine, sine = jnp.cos(angle), jnp.sin(angle)
    first = jnp.maximum(start, token - (WINDOW - 1))
    return (
        jnp.concatenate([cosine, cosine], axis=1),
        jnp.concatenate([-sine, sine], axis=1),
        first[:, None],
    )


def rotate(vectors, gain, cosine, sine):
    factor = lax.rsqrt(jnp.mean(vectors * vectors, axis=1, keepdims=True) + norm_eps)
    normed = vectors * factor * gain
    return normed * cosine + pltpu.roll(normed, HEAD_WIDTH // 2, 1) * sine


def rotate_back(grad, vectors, gain, cosine, sine):
    factor = lax.rsqrt(jnp.mean(vectors * vectors, axis=1, keepdims=True) + norm_eps)
    inner = (grad * cosine + pltpu.roll(grad * sine, HEAD_WIDTH // 2, 1)) * gain
    shared = jnp.mean(inner * vectors, axis=1, keepdims=True) * (factor * factor * factor)
    return inner * factor - vectors * shared


def head_kernel(planes, share, tokens_hbm, *refs):
    pieces = refs[: 2 * planes - 1]
    (cos_ref, sin_ref, first_ref, qgain_ref, kgain_ref, cot_ref) = refs[2 * planes - 1 : 2 * planes + 5]
    out_ref, grad_ref, weight_hbm = refs[2 * planes + 5 : 2 * planes + 8]
    (tok, weight, proj, query, key, value, key_sum, value_sum, piece_sem, tok_sem, weight_sem) = refs[
        2 * planes + 8 :
    ]
    length, rows = tok.shape[0], pieces[0].shape[0]
    blocks = length // QUERY_BLOCK
    mine = lax.axis_index("dp")

    def piece_copy(slot, place):
        at = pl.multiple_of(place * rows, 16)
        return pltpu.make_async_copy(
            pieces[slot], weight.at[pl.ds(at, rows)], piece_sem.at[slot]
        )

    def each_piece(act):
        act(piece_copy(0, mine))
        for step in range(1, planes):

            @pl.when(mine >= step)
            def _():
                act(piece_copy(step, mine - step))

            @pl.when(mine + step < planes)
            def _():
                act(piece_copy(planes - 1 + step, mine + step))

    def tok_copy(block):
        at = pl.ds(block * QUERY_BLOCK, QUERY_BLOCK)
        return pltpu.make_async_copy(tokens_hbm.at[at], tok.at[at], tok_sem.at[block])

    each_piece(lambda copy: copy.start())
    for block in range(blocks):
        tok_copy(block).start()
    each_piece(lambda copy: copy.wait())
    weight_copy = pltpu.make_async_copy(weight, weight_hbm, weight_sem)
    weight_copy.start()

    qgain, kgain = qgain_ref[...], kgain_ref[...]
    key_at, value_at = share * HEAD_WIDTH, (share + 1) * HEAD_WIDTH
    for block in range(blocks):
        tok_copy(block).wait()
        at = pl.ds(block * QUERY_BLOCK, QUERY_BLOCK)
        part = dot(tok[at, :], weight[...], NN)
        proj[at, :] = part
        cosine, sine = cos_ref[at, :], sin_ref[at, :]
        for head in range(share):
            cols = slice(head * HEAD_WIDTH, (head + 1) * HEAD_WIDTH)
            query[at, cols] = rotate(part[:, cols], qgain, cosine, sine).astype(jnp.bfloat16)
        key[at, :] = rotate(part[:, key_at:value_at], kgain, cosine, sine).astype(jnp.bfloat16)
        value[at, :] = part[:, value_at:].astype(jnp.bfloat16)

    key_sum[...] = jnp.zeros_like(key_sum)
    value_sum[...] = jnp.zeros_like(value_sum)
    for block in range(blocks):
        start = block * QUERY_BLOCK
        low = max(0, (start - (WINDOW - 1)) // QUERY_BLOCK * QUERY_BLOCK)
        width = start + QUERY_BLOCK - low
        at, keys_at = pl.ds(start, QUERY_BLOCK), pl.ds(low, width)
        key_token = low + lax.broadcasted_iota(jnp.int32, (QUERY_BLOCK, width), 1)
        query_token = start + lax.broadcasted_iota(jnp.int32, (QUERY_BLOCK, 1), 0)
        allowed = (key_token >= first_ref[at, :]) & (key_token <= query_token)
        key_part, value_part = key[keys_at, :], value[keys_at, :]
        cosine, sine = cos_ref[at, :], sin_ref[at, :]
        for head in range(share):
            cols = slice(head * HEAD_WIDTH, (head + 1) * HEAD_WIDTH)
            query_part, cot_part = query[at, cols], cot_ref[at, cols]
            scores = dot(query_part, key_part, NT) * score_scale
            weights = jnp.where(allowed, jnp.exp(scores), 0.0)
            probs = weights * (1.0 / jnp.sum(weights, axis=1, keepdims=True))
            probs_bf = probs.astype(jnp.bfloat16)
            out_ref[at, cols] = dot(probs_bf, value_part, NN).astype(jnp.bfloat16)
            value_sum[keys_at, :] += dot(probs_bf, cot_part, TN)
            grad_probs = dot(cot_part, value_part, NT)
            delta = jnp.sum(probs * grad_probs, axis=1, keepdims=True)
            grad_scores = (probs * (grad_probs - delta)).astype(jnp.bfloat16)
            key_sum[keys_at, :] += dot(grad_scores, query_part, TN)
            grad_query = dot(grad_scores, key_part, NN) * score_scale
            grad_ref[at, cols] = rotate_back(
                grad_query, proj[at, cols], qgain, cosine, sine
            ).astype(jnp.bfloat16)
    for block in range(blocks):
        at = pl.ds(block * QUERY_BLOCK, QUERY_BLOCK)
        grad_ref[at, key_at:value_at] = rotate_back(
            key_sum[at, :] * score_scale,
            proj[at, key_at:value_at],
            kgain,
            cos_ref[at, :],
            sin_ref[at, :],
        ).astype(jnp.bfloat16)
        grad_ref[at, value_at:] = value_sum[at, :].astype(jnp.bfloat16)
    weight_copy.wait()


def heads(planes, share, row_tokens, pieces, tables, gains, cot):
    length, model = row_tokens.shape
    width = pieces[0].shape[1]
    blocks = length // QUERY_BLOCK
    hbm = pl.BlockSpec(memory_space=pl.ANY)
    vmem = pl.BlockSpec(memory_space=pltpu.VMEM)
    return pl.pallas_call(
        functools.partial(head_kernel, planes, share),
        out_shape=(
            jax.ShapeDtypeStruct((length, share * HEAD_WIDTH), jnp.bfloat16),
            jax.ShapeDtypeStruct((length, width), jnp.bfloat16),
            jax.ShapeDtypeStruct((model, width), jnp.bfloat16),
        ),
        in_specs=[hbm] * (2 * planes) + [vmem] * 6,
        out_specs=(vmem, vmem, hbm),
        scratch_shapes=[
            pltpu.VMEM((length, model), jnp.bfloat16),
            pltpu.VMEM((model, width), jnp.bfloat16),
            pltpu.VMEM((length, width), jnp.float32),
            pltpu.VMEM((length, share * HEAD_WIDTH), jnp.bfloat16),
            pltpu.VMEM((length, HEAD_WIDTH), jnp.bfloat16),
            pltpu.VMEM((length, HEAD_WIDTH), jnp.bfloat16),
            pltpu.VMEM((length, HEAD_WIDTH), jnp.float32),
            pltpu.VMEM((length, HEAD_WIDTH), jnp.float32),
            pltpu.SemaphoreType.DMA((2 * planes - 1,)),
            pltpu.SemaphoreType.DMA((blocks,)),
            pltpu.SemaphoreType.DMA,
        ],
        compiler_params=pltpu.CompilerParams(vmem_limit_bytes=48 * 1024 * 1024),
        cost_estimate=pl.CostEstimate(
            flops=2 * length * model * width + 12 * share * length * length * HEAD_WIDTH,
            bytes_accessed=2 * (length * model + 2 * model * width + 4 * length * width),
            transcendentals=share * length * length,
        ),
        name="heads",
    )(row_tokens, *pieces, *tables, *gains, cot)


def token_kernel(groups, *refs):
    total = None
    for group in range(groups):
        term = dot(refs[group][...], refs[groups + group][...], NT)
        total = term if total is None else total + term
    refs[-1][...] = total.astype(jnp.bfloat16)


def token_terms(grads, weights):
    groups = len(grads)
    length, width = grads[0].shape
    model = weights[0].shape[0]
    return pl.pallas_call(
        functools.partial(token_kernel, groups),
        grid=(length // QUERY_BLOCK,),
        out_shape=jax.ShapeDtypeStruct((length, model), jnp.bfloat16),
        in_specs=[pl.BlockSpec((QUERY_BLOCK, width), lambda i: (i, 0))] * groups
        + [pl.BlockSpec((model, width), lambda i: (0, 0))] * groups,
        out_specs=pl.BlockSpec((QUERY_BLOCK, model), lambda i: (i, 0)),
        compiler_params=pltpu.CompilerParams(vmem_limit_bytes=48 * 1024 * 1024),
        cost_estimate=pl.CostEstimate(
            flops=2 * length * model * width * groups,
            bytes_accessed=2 * (length * model + groups * width * (length + model)),
            transcendentals=0,
        ),
        name="token_terms",
    )(*grads, *weights)


def gather_line(block, planes):
    left, right, from_left, from_right = block, block, [], []
    for step in range(1, planes):
        left = lax.ppermute(left, "dp", [(i, i + 1) for i in range(step - 1, planes - 1)])
        right = lax.ppermute(right, "dp", [(i, i - 1) for i in range(1, planes - step + 1)])
        from_left.append(left)
        from_right.append(right)
    return [block] + from_left + from_right


def local(planes, tokens, q_weight, key_projection, value_projection, q_gain, k_gain, doc_lengths, out_cot):
    value_heads = key_projection.shape[1] // HEAD_WIDTH
    share = q_weight.shape[1] // key_projection.shape[1]
    wide = share * HEAD_WIDTH
    row_tokens = lax.all_gather(tokens, "seq", axis=0, tiled=True)
    tables = doc_tables(doc_lengths[0], row_tokens.shape[0])
    gains = (q_gain[None, :], k_gain[None, :])
    outs, grads, weights, sums = [], [], [], []
    for group in range(value_heads):
        narrow = slice(group * HEAD_WIDTH, (group + 1) * HEAD_WIDTH)
        broad = slice(group * wide, (group + 1) * wide)
        block = jnp.concatenate(
            [q_weight[:, broad], key_projection[:, narrow], value_projection[:, narrow]], axis=1
        )
        out, grad, weight = heads(
            planes, share, row_tokens, gather_line(block, planes), tables, gains, out_cot[:, broad]
        )
        outs.append(out)
        grads.append(grad)
        weights.append(weight)
        sums.append(
            lax.psum_scatter(
                dot(row_tokens, grad, TN).astype(jnp.bfloat16), "dp", scatter_dimension=0, tiled=True
            )
        )
    attn_out = lax.all_to_all(
        jnp.concatenate(outs, axis=1), "seq", split_axis=0, concat_axis=1, tiled=True
    )
    token_grad = lax.psum_scatter(
        token_terms(grads, weights), "seq", scatter_dimension=0, tiled=True
    )

    def columns(first, count):
        return jnp.concatenate(
            [s[:, first : first + count].astype(jnp.float32) for s in sums], axis=1
        )

    return (
        attn_out,
        token_grad,
        columns(0, wide),
        columns(wide, HEAD_WIDTH),
        columns(wide + HEAD_WIDTH, HEAD_WIDTH),
    )


def solution(mesh):
    rows, split = P(("dp", "seq"), None), P("dp", "seq")
    return jax.shard_map(
        functools.partial(local, mesh.shape["dp"]),
        mesh=mesh,
        in_specs=(rows, split, split, split, P(), P(), P("dp", None), split),
        out_specs=(rows, rows, split, split, split),
        check_vma=False,
    )
```

```python
import functools

import jax
import jax.numpy as jnp
from jax import lax
from jax.experimental import pallas as pl
from jax.experimental.pallas import tpu as pltpu
from jax.sharding import PartitionSpec as P

HEAD_WIDTH = 128
WINDOW = 1024
QUERY_BLOCK = 256
SPLIT = True

score_scale = 168.0 ** (-0.5)
rope_base = 10000.0
log2_e = 1.4426950408889634
norm_eps = 1e-06
NN = (((1,), (0,)), ((), ()))
NT = (((1,), (1,)), ((), ()))
TN = (((0,), (0,)), ((), ()))


def dot(a, b, dims):
    return lax.dot_general(a, b, dims, preferred_element_type=jnp.float32)


def doc_tables(length_row, length):
    ends = jnp.cumsum(length_row, dtype=jnp.int32)
    starts = ends - length_row
    token = jnp.arange(length, dtype=jnp.int32)
    inside = (token[:, None] >= starts[None, :]) & (token[:, None] < ends[None, :])
    start = jnp.sum(jnp.where(inside, starts[None, :], 0), axis=1, dtype=jnp.int32)
    half = HEAD_WIDTH // 2
    inverse = rope_base ** (-jnp.arange(half, dtype=jnp.float32) * (2.0 / HEAD_WIDTH))
    angle = (token - start).astype(jnp.float32)[:, None] * inverse[None, :]
    cosine, sine = jnp.cos(angle), jnp.sin(angle)
    return (
        jnp.concatenate([cosine, cosine], axis=1),
        jnp.concatenate([-sine, sine], axis=1),
    )


def rotate(vectors, gain, cosine, sine):
    factor = lax.rsqrt(jnp.mean(vectors * vectors, axis=1, keepdims=True) + norm_eps)
    normed = vectors * factor * gain
    return normed * cosine + pltpu.roll(normed, HEAD_WIDTH // 2, 1) * sine


def rotate_back(grad, vectors, gain, cosine, sine):
    factor = lax.rsqrt(jnp.mean(vectors * vectors, axis=1, keepdims=True) + norm_eps)
    inner = (grad * cosine + pltpu.roll(grad * sine, HEAD_WIDTH // 2, 1)) * gain
    shared = jnp.mean(inner * vectors, axis=1, keepdims=True) * (factor * factor * factor)
    return inner * factor - vectors * shared


def first_keys(lengths_ref, query_token):
    first, end = jnp.maximum(query_token - (WINDOW - 1), 0), 0
    for document in range(lengths_ref.shape[1]):
        end = end + lengths_ref[0, document]
        first = jnp.maximum(first, jnp.where(query_token >= end, end, 0))
    return first


def head_kernel(planes, share, halves, marks, lengths_ref, qgain_ref, kgain_ref, *refs):
    count = halves * (2 * planes - 1)
    pieces = refs[:count]
    tokens_hbm, cos_hbm, sin_hbm, cot_hbm = refs[count : count + 4]
    refs = refs[count + 4 + marks :]
    out_ref, grad_ref, weight_hbm, terms_hbm = refs[:4]
    (tok, weight, cos_ref, sin_ref, cot_ref, proj, query, key, value, key_sum, value_sum, terms) = refs[4:16]
    piece_sem, tok_sem, small_sem, weight_sem, terms_sem = refs[16:]
    length, rows = tok.shape[0], pieces[0].shape[0]
    part_width = weight.shape[1] // halves
    blocks = length // QUERY_BLOCK
    mine = lax.axis_index("dp")

    def each_piece(act):
        for half in range(halves):
            first = half * (2 * planes - 1)
            cols = pl.ds(half * part_width, part_width)

            def copy(slot, place):
                at = pl.ds(pl.multiple_of(place * rows, 16), rows)
                act(
                    pltpu.make_async_copy(
                        pieces[first + slot], weight.at[at, cols], piece_sem.at[first + slot]
                    )
                )

            copy(0, mine)
            for step in range(1, planes):
                pl.when(mine >= step)(lambda: copy(step, mine - step))
                pl.when(mine + step < planes)(lambda: copy(planes - 1 + step, mine + step))

    def tok_copy(block):
        at = pl.ds(block * QUERY_BLOCK, QUERY_BLOCK)
        return pltpu.make_async_copy(tokens_hbm.at[at], tok.at[at], tok_sem.at[block])

    small = [
        pltpu.make_async_copy(source, target, small_sem.at[slot])
        for slot, (source, target) in enumerate(
            ((cos_hbm, cos_ref), (sin_hbm, sin_ref), (cot_hbm, cot_ref))
        )
    ]
    each_piece(lambda copy: copy.start())
    for block in range(blocks):
        tok_copy(block).start()
    for copy in small:
        copy.start()
    each_piece(lambda copy: copy.wait())
    weight_copy = pltpu.make_async_copy(weight, weight_hbm, weight_sem)
    weight_copy.start()

    qgain, kgain = qgain_ref[...], kgain_ref[...]
    key_at, value_at = share * HEAD_WIDTH, (share + 1) * HEAD_WIDTH
    for block in range(blocks):
        tok_copy(block).wait()
        if block == 0:
            for copy in small:
                copy.wait()
        at = pl.ds(block * QUERY_BLOCK, QUERY_BLOCK)
        part = dot(tok[at, :], weight[...], NN)
        proj[at, :] = part
        cosine, sine = cos_ref[at, :], sin_ref[at, :]
        for head in range(share):
            cols = slice(head * HEAD_WIDTH, (head + 1) * HEAD_WIDTH)
            query[at, cols] = rotate(part[:, cols], qgain, cosine, sine).astype(jnp.bfloat16)
        key[at, :] = rotate(part[:, key_at:value_at], kgain, cosine, sine).astype(jnp.bfloat16)
        value[at, :] = part[:, value_at:].astype(jnp.bfloat16)

    key_sum[...] = jnp.zeros_like(key_sum)
    value_sum[...] = jnp.zeros_like(value_sum)
    for block in range(blocks):
        start = block * QUERY_BLOCK
        low = max(0, (start - (WINDOW - 1)) // QUERY_BLOCK * QUERY_BLOCK)
        width = start + QUERY_BLOCK - low
        at, keys_at = pl.ds(start, QUERY_BLOCK), pl.ds(low, width)
        key_token = low + lax.broadcasted_iota(jnp.int32, (QUERY_BLOCK, width), 1)
        query_token = start + lax.broadcasted_iota(jnp.int32, (QUERY_BLOCK, 1), 0)
        allowed = (key_token >= first_keys(lengths_ref, query_token)) & (key_token <= query_token)
        key_part, value_part = key[keys_at, :], value[keys_at, :]
        cosine, sine = cos_ref[at, :], sin_ref[at, :]
        for head in range(share):
            cols = slice(head * HEAD_WIDTH, (head + 1) * HEAD_WIDTH)
            query_part, cot_part = query[at, cols], cot_ref[at, cols]
            scores = dot(query_part, key_part, NT) * (score_scale * log2_e)
            weights = jnp.where(allowed, jnp.exp2(scores), 0.0)
            probs = weights * (1.0 / jnp.sum(weights, axis=1, keepdims=True))
            probs_bf = probs.astype(jnp.bfloat16)
            mixed = dot(probs_bf, value_part, NN)
            out_ref[at, cols] = mixed.astype(jnp.bfloat16)
            value_sum[keys_at, :] += dot(probs_bf, cot_part, TN)
            grad_probs = dot(cot_part, value_part, NT)
            delta = jnp.sum(mixed * cot_part.astype(jnp.float32), axis=1, keepdims=True)
            grad_scores = (probs * (grad_probs - delta)).astype(jnp.bfloat16)
            key_sum[keys_at, :] += dot(grad_scores, query_part, TN)
            grad_query = dot(grad_scores, key_part, NN) * score_scale
            grad_ref[at, cols] = rotate_back(
                grad_query, proj[at, cols], qgain, cosine, sine
            ).astype(jnp.bfloat16)
    for block in range(blocks):
        at = pl.ds(block * QUERY_BLOCK, QUERY_BLOCK)
        grad_ref[at, key_at:value_at] = rotate_back(
            key_sum[at, :] * score_scale,
            proj[at, key_at:value_at],
            kgain,
            cos_ref[at, :],
            sin_ref[at, :],
        ).astype(jnp.bfloat16)
        grad_ref[at, value_at:] = value_sum[at, :].astype(jnp.bfloat16)

    grads = grad_ref[...]
    model = tok.shape[1]
    depth = model // terms_sem.shape[0]
    copies = []
    for part in range(terms_sem.shape[0]):
        at = pl.ds(part * depth, depth)
        terms[at, :] = dot(tok[:, at], grads, TN).astype(jnp.bfloat16)
        copies.append(pltpu.make_async_copy(terms.at[at], terms_hbm.at[at], terms_sem.at[part]))
        copies[-1].start()
    for copy in copies:
        copy.wait()
    weight_copy.wait()


def heads(planes, share, row_tokens, pieces, tables, gains, lengths, cot, marks):
    length, model = row_tokens.shape
    halves = len(pieces) // (2 * planes - 1)
    width = pieces[0].shape[1] * halves
    blocks = length // QUERY_BLOCK
    parts = max(k for k in (1, 3, 7) if model % (k * HEAD_WIDTH) == 0)
    hbm = pl.BlockSpec(memory_space=pltpu.HBM)
    vmem = pl.BlockSpec(memory_space=pltpu.VMEM)
    table = pltpu.VMEM((length, HEAD_WIDTH), jnp.float32)
    return pl.pallas_call(
        functools.partial(head_kernel, planes, share, halves, len(marks)),
        out_shape=(
            jax.ShapeDtypeStruct((length, share * HEAD_WIDTH), jnp.bfloat16),
            jax.ShapeDtypeStruct((length, width), jnp.bfloat16),
            jax.ShapeDtypeStruct((model, width), jnp.bfloat16),
            jax.ShapeDtypeStruct((model, width), jnp.bfloat16),
        ),
        in_specs=[pl.BlockSpec(memory_space=pltpu.SMEM), vmem, vmem]
        + [hbm] * (len(pieces) + 4 + len(marks)),
        out_specs=(vmem, vmem, hbm, hbm),
        scratch_shapes=[
            pltpu.VMEM((length, model), jnp.bfloat16),
            pltpu.VMEM((model, width), jnp.bfloat16),
            table,
            table,
            pltpu.VMEM((length, share * HEAD_WIDTH), jnp.bfloat16),
            pltpu.VMEM((length, width), jnp.float32),
            pltpu.VMEM((length, share * HEAD_WIDTH), jnp.bfloat16),
            pltpu.VMEM((length, HEAD_WIDTH), jnp.bfloat16),
            pltpu.VMEM((length, HEAD_WIDTH), jnp.bfloat16),
            table,
            table,
            pltpu.VMEM((model, width), jnp.bfloat16),
            pltpu.SemaphoreType.DMA((len(pieces),)),
            pltpu.SemaphoreType.DMA((blocks,)),
            pltpu.SemaphoreType.DMA((3,)),
            pltpu.SemaphoreType.DMA,
            pltpu.SemaphoreType.DMA((parts,)),
        ],
        compiler_params=pltpu.CompilerParams(vmem_limit_bytes=60 * 1024 * 1024),
        cost_estimate=pl.CostEstimate(
            flops=4 * length * model * width + 12 * share * length * length * HEAD_WIDTH,
            bytes_accessed=2 * (length * model + 3 * model * width + 4 * length * width),
            transcendentals=share * length * length,
        ),
        name="heads",
    )(lengths, *gains, *pieces, row_tokens, *tables, cot, *marks)


def token_kernel(adds, marks, side_ref, grad_ref, weight_ref, *refs):
    grad, out_ref = grad_ref[...], refs[-1]
    grad = grad.reshape(grad.shape[0] * grad.shape[1], grad.shape[2])
    total = dot(grad, weight_ref[...], NT).reshape(out_ref.shape)
    for index in range(adds):
        total = total + refs[index][...].astype(jnp.float32)
    out_ref[...] = total.astype(jnp.bfloat16)


def token_terms(grad, weight, side, owners, adds, marks):
    length, width = grad.shape
    model = weight.shape[0]
    rows, pairs = length // owners, owners // 2
    batch = 2 if pairs % 2 == 0 else 1
    block = pl.BlockSpec((batch, rows, model), lambda i, side_ref: (i, 0, 0))
    return pl.pallas_call(
        functools.partial(token_kernel, len(adds), len(marks)),
        grid_spec=pltpu.PrefetchScalarGridSpec(
            num_scalar_prefetch=1,
            grid=(pairs // batch,),
            in_specs=[
                pl.BlockSpec(
                    (batch, None, rows, width), lambda i, side_ref: (i, side_ref[0], 0, 0)
                ),
                pl.BlockSpec((model, width), lambda i, side_ref: (0, 0)),
            ]
            + [block] * len(adds)
            + [pl.BlockSpec(memory_space=pltpu.HBM)] * len(marks),
            out_specs=block,
        ),
        out_shape=jax.ShapeDtypeStruct((pairs, rows, model), jnp.bfloat16),
        compiler_params=pltpu.CompilerParams(vmem_limit_bytes=60 * 1024 * 1024),
        cost_estimate=pl.CostEstimate(
            flops=length * width, bytes_accessed=length * width, transcendentals=0
        ),
        name="token_terms",
    )(side.reshape(1), grad.reshape(pairs, 2, rows, width), weight, *adds, *marks)


def step_kernel(planes, given, gathers, adds, marks, terms_hbm, *refs):
    taken, received = refs[: 2 * gathers], refs[2 * gathers : 2 * gathers + 2 * adds]
    refs = refs[2 * gathers + 2 * adds + marks :]
    outs, owns, others, sem = refs[:2], refs[2:4], refs[4:6], refs[6]
    mine = lax.axis_index("dp")
    scatters = (mine < given, mine >= planes - given)
    places = (planes - given + mine, mine - (planes - given))

    def copies(way):
        found = [pltpu.make_async_copy(terms_hbm.at[places[way]], owns[way], sem.at[way, 0])]
        if adds:
            found.append(pltpu.make_async_copy(received[way], others[way], sem.at[way, 1]))
        return found

    def passing(way):
        return pltpu.make_async_copy(taken[way], outs[way], sem.at[way, 2])

    for way in range(2):

        @pl.when(scatters[way])
        def _():
            for copy in copies(way):
                copy.start()

        if gathers:

            @pl.when(jnp.logical_not(scatters[way]))
            def _():
                passing(way).start()

    for way in range(2):

        @pl.when(scatters[way])
        def _():
            for copy in copies(way):
                copy.wait()
            total = owns[way][...]
            if adds:
                total = total.astype(jnp.float32) + others[way][...].astype(jnp.float32)
            outs[way][...] = total.astype(jnp.bfloat16)

        if gathers:

            @pl.when(jnp.logical_not(scatters[way]))
            def _():
                passing(way).wait()


def step_terms(planes, given, terms, taken, received, marks):
    shape = terms.shape[1:]
    hbm = pl.BlockSpec(memory_space=pltpu.HBM)
    vmem = pl.BlockSpec(memory_space=pltpu.VMEM)
    return pl.pallas_call(
        functools.partial(
            step_kernel, planes, given, len(taken) // 2, len(received) // 2, len(marks)
        ),
        out_shape=(jax.ShapeDtypeStruct(shape, jnp.bfloat16),) * 2,
        in_specs=[hbm] * (1 + len(taken) + len(received) + len(marks)),
        out_specs=(vmem, vmem),
        scratch_shapes=[pltpu.VMEM(shape, jnp.bfloat16)] * 4 + [pltpu.SemaphoreType.DMA((2, 3))],
        compiler_params=pltpu.CompilerParams(vmem_limit_bytes=60 * 1024 * 1024),
        cost_estimate=pl.CostEstimate(flops=1, bytes_accessed=1, transcendentals=0),
        name="step_terms",
    )(terms, *taken, *received, *marks)


def total_kernel(groups, share, *refs):
    outs, pieces, sem = refs[3 * groups : 3 * groups + 3], refs[3 * groups + 3 : -1], refs[-1]
    mine = lax.axis_index("dp")
    copies = []
    for group in range(groups):
        sources = (refs[3 * group].at[mine], refs[3 * group + 1], refs[3 * group + 2])
        for index, source in enumerate(sources):
            slot = 3 * group + index
            copies.append(pltpu.make_async_copy(source, pieces[slot], sem.at[slot]))
            copies[-1].start()
    wide = share * HEAD_WIDTH
    for group in range(groups):
        for index in range(3):
            copies[3 * group + index].wait()
        total = sum(pieces[3 * group + index][...].astype(jnp.float32) for index in range(3))
        outs[0][:, group * wide : (group + 1) * wide] = total[:, :wide]
        narrow = slice(group * HEAD_WIDTH, (group + 1) * HEAD_WIDTH)
        outs[1][:, narrow] = total[:, wide : wide + HEAD_WIDTH]
        outs[2][:, narrow] = total[:, wide + HEAD_WIDTH :]


def total_terms(share, parts):
    groups = len(parts)
    rows, width = parts[0][1].shape
    hbm = pl.BlockSpec(memory_space=pltpu.HBM)
    vmem = pl.BlockSpec(memory_space=pltpu.VMEM)
    return pl.pallas_call(
        functools.partial(total_kernel, groups, share),
        out_shape=tuple(
            jax.ShapeDtypeStruct((rows, groups * count * HEAD_WIDTH), jnp.float32)
            for count in (share, 1, 1)
        ),
        in_specs=[hbm] * (3 * groups),
        out_specs=(vmem,) * 3,
        scratch_shapes=[pltpu.VMEM((rows, width), jnp.bfloat16)] * (3 * groups)
        + [pltpu.SemaphoreType.DMA((3 * groups,))],
        compiler_params=pltpu.CompilerParams(vmem_limit_bytes=60 * 1024 * 1024),
        cost_estimate=pl.CostEstimate(flops=1, bytes_accessed=1, transcendentals=0),
        name="total_terms",
    )(*[array for part in parts for array in part])


def after(value, *others):
    return lax.optimization_barrier((value, *others))[0]


def up(value, first, last):
    return lax.ppermute(value, "dp", [(i, i + 1) for i in range(first, last)])


def down(value, first, last):
    return lax.ppermute(value, "dp", [(i + 1, i) for i in range(first, last)])


def add(*terms):
    return functools.reduce(lambda a, b: a + b, [term.astype(jnp.float32) for term in terms])


class Line:
    def __init__(self, planes):
        self.planes = planes

    def gather(self, block):
        self.block, self.left, self.right = block, [], []

    def gather_step(self):
        done, last = len(self.left), self.planes - 1
        left = self.left[-1] if done else self.block
        right = self.right[-1] if done else self.block
        self.left.append(up(left, done, last))
        self.right.append(down(right, 0, last - done))

    def pieces(self):
        return [self.block] + self.left + self.right

    def scatter(self, terms):
        self.terms = terms.reshape(self.planes, terms.shape[0] // self.planes, terms.shape[1])
        self.given, self.received = 0, ()

    def scatter_step(self, gathers, *marks):
        self.given += 1
        taken = (self.left[-1], self.right[-1]) if gathers else ()
        left, right = step_terms(
            self.planes, self.given, self.terms, taken, self.received, marks
        )
        last = self.planes - 1
        count = last if gathers else self.given
        self.received = up(left, 0, count), down(right, last - count, last)
        if gathers:
            self.left.append(self.received[0])
            self.right.append(self.received[1])
        return left, right


def local(planes, owners, tokens, q_weight, key_projection, value_projection, q_gain, k_gain, doc_lengths, out_cot):
    groups = key_projection.shape[1] // HEAD_WIDTH
    share = q_weight.shape[1] // key_projection.shape[1]
    wide = share * HEAD_WIDTH
    steps = planes - 1
    row_tokens = lax.all_gather(tokens, "seq", axis=0, tiled=True)
    length, model = row_tokens.shape
    rows = length // owners
    tables = doc_tables(doc_lengths[0], length)
    gains = (q_gain[None, :], k_gain[None, :])
    me = lax.axis_index("seq")
    side, pair = lax.rem(me, 2), lax.div(me, 2)

    def halves(group):
        narrow = slice(group * HEAD_WIDTH, (group + 1) * HEAD_WIDTH)
        broad = slice(group * wide, (group + 1) * wide)
        return (
            q_weight[:, broad],
            jnp.concatenate([key_projection[:, narrow], value_projection[:, narrow]], axis=1),
        )

    pieces = []
    if SPLIT and wide == 2 * HEAD_WIDTH:
        lines = [Line(planes), Line(planes)]
        for line, half in zip(lines, halves(0)):
            line.gather(half)
        for _ in range(steps):
            for line in lines:
                line.gather_step()
        for line in lines:
            pieces += line.pieces()
    else:
        line = Line(planes)
        line.gather(jnp.concatenate(halves(0), axis=1))
        for _ in range(steps):
            line.gather_step()
        pieces = line.pieces()
    arrived = (line.left[-1], line.right[-1])
    spread, parts, marks = [], [], ()
    sent = kept = ()
    for group in range(groups):
        final = group + 1 == groups
        if not final:
            following = Line(planes)
            following.gather(after(jnp.concatenate(halves(group + 1), axis=1), *arrived))
            following.gather_step()
        out, grad, weight, terms = heads(
            planes, share, row_tokens, pieces, tables, gains, doc_lengths,
            out_cot[:, group * wide : (group + 1) * wide], marks,
        )
        spread.append(lax.all_to_all(out, "seq", split_axis=0, concat_axis=0, tiled=True))
        if not final:
            following.scatter(terms)
            first = following.scatter_step(steps > 1)
            sent = (token_terms(grad, weight, 1 - side, owners, sent, first),)
            marks = sent
            for _ in range(1, steps - 1):
                marks = following.scatter_step(True, *marks)
            kept = (token_terms(grad, weight, side, owners, kept, marks),)
            ended = following.scatter_step(False, *kept) if steps > 1 else ()
            parts.append((following.terms, *following.received))
            marks = (*ended, spread[-1])
            pieces = following.pieces()
            arrived = ()
    sent = token_terms(grad, weight, 1 - side, owners, sent, parts[-1][1:] if parts else ())
    received = lax.ppermute(sent, "seq", [(i, i ^ 1) for i in range(owners)])
    line = Line(planes)
    line.scatter(terms)
    first = line.scatter_step(False, sent)
    kept = token_terms(grad, weight, side, owners, (*kept, received), (*first, spread[-1]))
    shares = [lax.dynamic_index_in_dim(kept, pair, 0, keepdims=False)]
    for other in range(1, owners // 2):
        part = lax.dynamic_index_in_dim(kept, pair ^ other, 0, keepdims=False)
        shares.append(lax.ppermute(part, "seq", [(i, i ^ (2 * other)) for i in range(owners)]))
    marks = (kept,)
    for _ in range(1, steps):
        marks = line.scatter_step(False, *marks)
    parts.append((line.terms, *line.received))
    token_grad = add(*shares).astype(jnp.bfloat16)
    attn_out = jnp.concatenate([part.reshape(owners, rows, wide) for part in spread], axis=2)
    attn_out = attn_out.transpose(1, 0, 2).reshape(rows, owners * groups * wide)
    return (attn_out, token_grad, *total_terms(share, parts))


def solution(mesh):
    rows, split = P(("dp", "seq"), None), P("dp", "seq")
    return jax.shard_map(
        functools.partial(local, mesh.shape["dp"], mesh.shape["seq"]),
        mesh=mesh,
        in_specs=(rows, split, split, split, P(), P(), P("dp", None), split),
        out_specs=(rows, rows, split, split, split),
        check_vma=False,
    )
```

```python
import functools

import jax
import jax.numpy as jnp
from jax import lax
from jax.experimental import pallas as pl
from jax.experimental.pallas import tpu as pltpu
from jax.sharding import PartitionSpec as P

HEAD_WIDTH = 128
WINDOW = 1024
QUERY_BLOCK = 256

score_scale = 168.0 ** (-0.5)
rope_base = 10000.0
log2_e = 1.4426950408889634
norm_eps = 1e-06
NN = (((1,), (0,)), ((), ()))
NT = (((1,), (1,)), ((), ()))
TN = (((0,), (0,)), ((), ()))


def dot(a, b, dims):
    return lax.dot_general(a, b, dims, preferred_element_type=jnp.float32)


def doc_tables(length_row, length):
    ends = jnp.cumsum(length_row, dtype=jnp.int32)
    starts = ends - length_row
    token = jnp.arange(length, dtype=jnp.int32)
    inside = (token[:, None] >= starts[None, :]) & (token[:, None] < ends[None, :])
    start = jnp.sum(jnp.where(inside, starts[None, :], 0), axis=1, dtype=jnp.int32)
    half = HEAD_WIDTH // 2
    inverse = rope_base ** (-jnp.arange(half, dtype=jnp.float32) * (2.0 / HEAD_WIDTH))
    angle = (token - start).astype(jnp.float32)[:, None] * inverse[None, :]
    cosine, sine = jnp.cos(angle), jnp.sin(angle)
    return (
        jnp.concatenate([cosine, cosine], axis=1),
        jnp.concatenate([-sine, sine], axis=1),
    )


def rotate(vectors, gain, cosine, sine):
    factor = lax.rsqrt(jnp.mean(vectors * vectors, axis=1, keepdims=True) + norm_eps)
    normed = vectors * factor * gain
    return normed * cosine + pltpu.roll(normed, HEAD_WIDTH // 2, 1) * sine


def rotate_back(grad, vectors, gain, cosine, sine):
    factor = lax.rsqrt(jnp.mean(vectors * vectors, axis=1, keepdims=True) + norm_eps)
    inner = (grad * cosine + pltpu.roll(grad * sine, HEAD_WIDTH // 2, 1)) * gain
    shared = jnp.mean(inner * vectors, axis=1, keepdims=True) * (factor * factor * factor)
    return inner * factor - vectors * shared


def first_keys(lengths_ref, query_token):
    first, end = jnp.maximum(query_token - (WINDOW - 1), 0), 0
    for document in range(lengths_ref.shape[1]):
        end = end + lengths_ref[0, document]
        first = jnp.maximum(first, jnp.where(query_token >= end, end, 0))
    return first


def head_kernel(share, halves, spots, marks, lengths_ref, qgain_ref, kgain_ref, *refs):
    count = len(spots)
    pieces = refs[:count]
    tokens_hbm, cos_hbm, sin_hbm, cot_hbm = refs[count : count + 4]
    refs = refs[count + 4 + marks :]
    out_ref, grad_ref, weight_hbm, terms_hbm = refs[:4]
    (tok, weight, cos_ref, sin_ref, cot_ref, proj, query, key, value, key_sum, value_sum, terms) = refs[4:16]
    piece_sem, tok_sem, small_sem, weight_sem, terms_sem = refs[16:]
    length, rows = tok.shape[0], pieces[0].shape[0]
    part_width = weight.shape[1] // halves
    blocks = length // QUERY_BLOCK
    mine = lax.axis_index("dp")

    def each_piece(act):
        for index, planes in enumerate(spots):
            half = index * halves // count
            cols = pl.ds(half * part_width, part_width)
            place = functools.reduce(
                lambda other, spot: jnp.where(mine == spot[0], spot[1], other), planes, 0
            )
            here = functools.reduce(
                lambda other, spot: other | (mine == spot[0]), planes[1:], mine == planes[0][0]
            )

            @pl.when(here)
            def _():
                at = pl.ds(pl.multiple_of(place * rows, 16), rows)
                act(pltpu.make_async_copy(pieces[index], weight.at[at, cols], piece_sem.at[index]))

    def tok_copy(block):
        at = pl.ds(pl.multiple_of(block * QUERY_BLOCK, QUERY_BLOCK), QUERY_BLOCK)
        return pltpu.make_async_copy(tokens_hbm.at[at], tok.at[at], tok_sem.at[block])

    small = [
        pltpu.make_async_copy(source, target, small_sem.at[slot])
        for slot, (source, target) in enumerate(
            ((cos_hbm, cos_ref), (sin_hbm, sin_ref), (cot_hbm, cot_ref))
        )
    ]
    each_piece(lambda copy: copy.start())
    for block in range(blocks):
        tok_copy(block).start()
    for copy in small:
        copy.start()
    each_piece(lambda copy: copy.wait())
    weight_copy = pltpu.make_async_copy(weight, weight_hbm, weight_sem)
    weight_copy.start()

    qgain, kgain = qgain_ref[...], kgain_ref[...]
    key_at, value_at = share * HEAD_WIDTH, (share + 1) * HEAD_WIDTH
    for copy in small:
        copy.wait()

    @pl.loop(0, blocks)
    def _(block):
        tok_copy(block).wait()
        at = pl.ds(pl.multiple_of(block * QUERY_BLOCK, QUERY_BLOCK), QUERY_BLOCK)
        part = dot(tok[at, :], weight[...], NN)
        proj[at, :] = part
        cosine, sine = cos_ref[at, :], sin_ref[at, :]
        for head in range(share):
            cols = slice(head * HEAD_WIDTH, (head + 1) * HEAD_WIDTH)
            query[at, cols] = rotate(part[:, cols], qgain, cosine, sine).astype(jnp.bfloat16)
        key[at, :] = rotate(part[:, key_at:value_at], kgain, cosine, sine).astype(jnp.bfloat16)
        value[at, :] = part[:, value_at:].astype(jnp.bfloat16)

    key_sum[...] = jnp.zeros_like(key_sum)
    value_sum[...] = jnp.zeros_like(value_sum)
    for block in range(blocks):
        start = block * QUERY_BLOCK
        low = max(0, (start - (WINDOW - 1)) // QUERY_BLOCK * QUERY_BLOCK)
        width = start + QUERY_BLOCK - low
        at, keys_at = pl.ds(start, QUERY_BLOCK), pl.ds(low, width)
        key_token = low + lax.broadcasted_iota(jnp.int32, (QUERY_BLOCK, width), 1)
        query_token = start + lax.broadcasted_iota(jnp.int32, (QUERY_BLOCK, 1), 0)
        allowed = (key_token >= first_keys(lengths_ref, query_token)) & (key_token <= query_token)
        key_part, value_part = key[keys_at, :], value[keys_at, :]
        cosine, sine = cos_ref[at, :], sin_ref[at, :]
        for head in range(share):
            cols = slice(head * HEAD_WIDTH, (head + 1) * HEAD_WIDTH)
            query_part, cot_part = query[at, cols], cot_ref[at, cols]
            scores = dot(query_part, key_part, NT) * (score_scale * log2_e)
            weights = jnp.where(allowed, jnp.exp2(scores), 0.0)
            probs = weights * (1.0 / jnp.sum(weights, axis=1, keepdims=True))
            probs_bf = probs.astype(jnp.bfloat16)
            mixed = dot(probs_bf, value_part, NN)
            out_ref[at, cols] = mixed.astype(jnp.bfloat16)
            value_sum[keys_at, :] += dot(probs_bf, cot_part, TN)
            grad_probs = dot(cot_part, value_part, NT)
            delta = jnp.sum(mixed * cot_part.astype(jnp.float32), axis=1, keepdims=True)
            grad_scores = (probs * (grad_probs - delta)).astype(jnp.bfloat16)
            key_sum[keys_at, :] += dot(grad_scores, query_part, TN)
            grad_query = dot(grad_scores, key_part, NN) * score_scale
            grad_ref[at, cols] = rotate_back(
                grad_query, proj[at, cols], qgain, cosine, sine
            ).astype(jnp.bfloat16)
    for block in range(blocks):
        at = pl.ds(block * QUERY_BLOCK, QUERY_BLOCK)
        grad_ref[at, key_at:value_at] = rotate_back(
            key_sum[at, :] * score_scale,
            proj[at, key_at:value_at],
            kgain,
            cos_ref[at, :],
            sin_ref[at, :],
        ).astype(jnp.bfloat16)
        grad_ref[at, value_at:] = value_sum[at, :].astype(jnp.bfloat16)

    grads = grad_ref[...]
    model = tok.shape[1]
    depth = model // terms_sem.shape[0]

    def terms_copy(part):
        at = pl.ds(pl.multiple_of(part * depth, HEAD_WIDTH), depth)
        return pltpu.make_async_copy(terms.at[at], terms_hbm.at[at], terms_sem.at[part])

    @pl.loop(0, terms_sem.shape[0])
    def _(part):
        at = pl.ds(pl.multiple_of(part * depth, HEAD_WIDTH), depth)
        terms[at, :] = dot(tok[:, at], grads, TN).astype(jnp.bfloat16)
        terms_copy(part).start()

    @pl.loop(0, terms_sem.shape[0])
    def _(part):
        terms_copy(part).wait()

    weight_copy.wait()


def heads(share, halves, pieces, spots, row_tokens, tables, gains, lengths, cot, marks):
    length, model = row_tokens.shape
    width = pieces[0].shape[1] * halves
    blocks = length // QUERY_BLOCK
    parts = max(k for k in (1, 3, 7) if model % (k * HEAD_WIDTH) == 0)
    hbm = pl.BlockSpec(memory_space=pltpu.HBM)
    vmem = pl.BlockSpec(memory_space=pltpu.VMEM)
    table = pltpu.VMEM((length, HEAD_WIDTH), jnp.float32)
    return pl.pallas_call(
        functools.partial(head_kernel, share, halves, spots, len(marks)),
        out_shape=(
            jax.ShapeDtypeStruct((length, share * HEAD_WIDTH), jnp.bfloat16),
            jax.ShapeDtypeStruct((length, width), jnp.bfloat16),
            jax.ShapeDtypeStruct((model, width), jnp.bfloat16),
            jax.ShapeDtypeStruct((model, width), jnp.bfloat16),
        ),
        in_specs=[pl.BlockSpec(memory_space=pltpu.SMEM), vmem, vmem]
        + [hbm] * (len(pieces) + 4 + len(marks)),
        out_specs=(vmem, vmem, hbm, hbm),
        scratch_shapes=[
            pltpu.VMEM((length, model), jnp.bfloat16),
            pltpu.VMEM((model, width), jnp.bfloat16),
            table,
            table,
            pltpu.VMEM((length, share * HEAD_WIDTH), jnp.bfloat16),
            pltpu.VMEM((length, width), jnp.float32),
            pltpu.VMEM((length, share * HEAD_WIDTH), jnp.bfloat16),
            pltpu.VMEM((length, HEAD_WIDTH), jnp.bfloat16),
            pltpu.VMEM((length, HEAD_WIDTH), jnp.bfloat16),
            table,
            table,
            pltpu.VMEM((model, width), jnp.bfloat16),
            pltpu.SemaphoreType.DMA((len(pieces),)),
            pltpu.SemaphoreType.DMA((blocks,)),
            pltpu.SemaphoreType.DMA((3,)),
            pltpu.SemaphoreType.DMA,
            pltpu.SemaphoreType.DMA((parts,)),
        ],
        compiler_params=pltpu.CompilerParams(vmem_limit_bytes=65024 * 1024),
        cost_estimate=pl.CostEstimate(
            flops=4 * length * model * width + 12 * share * length * length * HEAD_WIDTH,
            bytes_accessed=2 * (length * model + 3 * model * width + 4 * length * width),
            transcendentals=share * length * length,
        ),
        name="heads",
    )(lengths, *gains, *pieces, row_tokens, *tables, cot, *marks)


def token_kernel(adds, parts, marks, side_ref, grad_ref, weight_ref, *refs):
    grad = grad_ref[...]
    batch, rows = grad.shape[:2]
    grad = grad.reshape(batch * rows, grad.shape[2])
    total = dot(grad, weight_ref[...], NT).reshape(batch, rows, weight_ref.shape[0])
    for index in range(adds):
        total = total + refs[index][...].astype(jnp.float32)
    pieces, outs = refs[adds : adds + parts], refs[adds + parts + marks :]
    if not parts and len(outs) == 1:
        outs[0][...] = total.astype(jnp.bfloat16)
        return
    count = parts or len(outs)
    for place in range(count):

        @pl.when(pl.program_id(0) == place // batch)
        def _():
            row = total[place % batch]
            if parts:
                row = row + pieces[place][...].astype(jnp.float32)
                outs[0][place % batch] = row.astype(jnp.bfloat16)
            else:
                outs[place][...] = row.astype(jnp.bfloat16)


def token_terms(grad, weight, side, owners, adds, parts, marks, split):
    length, width = grad.shape
    model = weight.shape[0]
    rows, pairs = length // owners, owners // 2
    batch = 2 if pairs % 2 == 0 else 1
    block = pl.BlockSpec((batch, rows, model), lambda i, side_ref: (i, 0, 0))
    single = pl.BlockSpec((rows, model), lambda i, side_ref: (0, 0))
    out_specs, out_shape = block, jax.ShapeDtypeStruct((pairs, rows, model), jnp.bfloat16)
    if split:
        out_specs = (single,) * pairs
        out_shape = (jax.ShapeDtypeStruct((rows, model), jnp.bfloat16),) * pairs
    return pl.pallas_call(
        functools.partial(token_kernel, len(adds), len(parts), len(marks)),
        grid_spec=pltpu.PrefetchScalarGridSpec(
            num_scalar_prefetch=1,
            grid=(pairs // batch,),
            in_specs=[
                pl.BlockSpec(
                    (batch, None, rows, width), lambda i, side_ref: (i, side_ref[0], 0, 0)
                ),
                pl.BlockSpec((model, width), lambda i, side_ref: (0, 0)),
            ]
            + [block] * len(adds)
            + [single] * len(parts)
            + [pl.BlockSpec(memory_space=pltpu.HBM)] * len(marks),
            out_specs=out_specs,
        ),
        out_shape=out_shape,
        compiler_params=pltpu.CompilerParams(vmem_limit_bytes=65024 * 1024),
        cost_estimate=pl.CostEstimate(
            flops=length * width, bytes_accessed=length * width, transcendentals=0
        ),
        name="token_terms",
    )(side.reshape(1), grad.reshape(pairs, 2, rows, width), weight, *adds, *parts, *marks)


def mix_kernel(outs, count, marks, *refs):
    sources, refs = refs[:count], refs[count + marks :]
    targets, extra, sem = refs[: len(outs)], refs[len(outs) : -1], refs[-1]
    mine = lax.axis_index("dp")

    def each(act):
        for index, cases in enumerate(outs):
            for low, high, terms in cases:
                copies = []

                @pl.when((mine >= low) & (mine < high))
                def _():
                    for slot, (source, place) in enumerate(terms):
                        ref = sources[source]
                        ref = ref if place is None else ref.at[mine + place]
                        target = targets[index] if slot == 0 else extra[index]
                        copies.append(pltpu.make_async_copy(ref, target, sem.at[index, slot]))
                    act(index, copies)

    def start(index, copies):
        for copy in copies:
            copy.start()

    def finish(index, copies):
        for copy in copies:
            copy.wait()
        if len(copies) > 1:
            total = targets[index][...].astype(jnp.float32) + extra[index][...].astype(jnp.float32)
            targets[index][...] = total.astype(jnp.bfloat16)

    each(start)
    each(finish)


def mix(outs, sources, marks):
    shape = sources[0].shape[-2:]
    plain = pl.BlockSpec(memory_space=pl.ANY)
    vmem = pl.BlockSpec(memory_space=pltpu.VMEM)
    return pl.pallas_call(
        functools.partial(mix_kernel, outs, len(sources), len(marks)),
        out_shape=(jax.ShapeDtypeStruct(shape, jnp.bfloat16),) * len(outs),
        in_specs=[plain] * (len(sources) + len(marks)),
        out_specs=(vmem,) * len(outs),
        scratch_shapes=[pltpu.VMEM(shape, jnp.bfloat16)] * len(outs)
        + [pltpu.SemaphoreType.DMA((len(outs), 2))],
        compiler_params=pltpu.CompilerParams(vmem_limit_bytes=65024 * 1024),
        cost_estimate=pl.CostEstimate(flops=1, bytes_accessed=1, transcendentals=0),
        name="mix",
    )(*sources, *marks)


def scatter_cases(planes, step, terms, received_up, received_down):
    first, last = planes - step, step - planes
    ups = [(0, 1, [(terms, first)]), (1, step, [(terms, first), (received_up, None)])]
    downs = [
        (planes - 1, planes, [(terms, last)]),
        (planes - step, planes - 1, [(terms, last), (received_down, None)]),
    ]
    return ups, downs


def total_kernel(share, layout, count, *refs):
    sources, outs, pieces, sem = refs[:count], refs[count : count + 3], refs[count + 3 : -1], refs[-1]
    mine = lax.axis_index("dp")

    def each(act):
        for index, cases in enumerate(layout):
            for low, high, source, own in cases:

                @pl.when((mine >= low) & (mine < high))
                def _():
                    ref = sources[source].at[mine] if own else sources[source]
                    act(pltpu.make_async_copy(ref, pieces[index], sem.at[index]))

    each(lambda copy: copy.start())
    each(lambda copy: copy.wait())
    wide = share * HEAD_WIDTH
    for group in range(len(layout) // 3):
        total = sum(pieces[3 * group + index][...].astype(jnp.float32) for index in range(3))
        outs[0][:, group * wide : (group + 1) * wide] = total[:, :wide]
        narrow = slice(group * HEAD_WIDTH, (group + 1) * HEAD_WIDTH)
        outs[1][:, narrow] = total[:, wide : wide + HEAD_WIDTH]
        outs[2][:, narrow] = total[:, wide + HEAD_WIDTH :]


def total_terms(share, layout, sources):
    groups = len(layout) // 3
    rows, width = sources[0].shape[-2:]
    plain = pl.BlockSpec(memory_space=pl.ANY)
    vmem = pl.BlockSpec(memory_space=pltpu.VMEM)
    return pl.pallas_call(
        functools.partial(total_kernel, share, layout, len(sources)),
        out_shape=tuple(
            jax.ShapeDtypeStruct((rows, groups * count * HEAD_WIDTH), jnp.float32)
            for count in (share, 1, 1)
        ),
        in_specs=[plain] * len(sources),
        out_specs=(vmem,) * 3,
        scratch_shapes=[pltpu.VMEM((rows, width), jnp.bfloat16)] * len(layout)
        + [pltpu.SemaphoreType.DMA((len(layout),))],
        compiler_params=pltpu.CompilerParams(vmem_limit_bytes=65024 * 1024),
        cost_estimate=pl.CostEstimate(flops=1, bytes_accessed=1, transcendentals=0),
        name="total_terms",
    )(*sources)


def after(value, *others):
    return lax.optimization_barrier((value, *others))[0]


def up(value, first, last):
    return lax.ppermute(value, "dp", [(i, i + 1) for i in range(first, last)])


def down(value, first, last):
    return lax.ppermute(value, "dp", [(i + 1, i) for i in range(first, last)])


def add(*terms):
    return functools.reduce(lambda a, b: a + b, [term.astype(jnp.float32) for term in terms])


def link(value, *pairs):
    return lax.ppermute(value, "dp", pairs)


ENDS = ((0, 1), (3, 2))
OUTER = ((0, 1), (1, 0), (2, 3), (3, 2))
INNER = ((1, 2), (2, 1))
OUTWARD = ((1, 0), (2, 3))


def gather_four(parts):
    outer = [link(part, *OUTER) for part in parts]
    inner = [link(part, *INNER) for part in parts]
    inner_second = [link(part, *INNER) for part in outer]
    outer_second = [link(part, *OUTWARD) for part in inner]
    outer_third = [link(part, *OUTWARD) for part in inner_second]
    own = tuple((plane, plane) for plane in range(4))
    swap = tuple((plane, plane ^ 1) for plane in range(4))
    spots = (own, swap, ((1, 2), (2, 1)), ((1, 3), (2, 0)), ((0, 2), (3, 1)), ((0, 3), (3, 0)))
    columns = zip(parts, outer, inner, inner_second, outer_second, outer_third)
    return [piece for column in columns for piece in column], spots * len(parts)


def gather_line(block, planes):
    left, right = [block], [block]
    for step in range(planes - 1):
        left.append(up(left[-1], step, planes - 1))
        right.append(down(right[-1], 0, planes - 1 - step))
    spots = [tuple((plane, plane - hop) for plane in range(hop, planes)) for hop in range(planes)]
    spots += [
        tuple((plane, plane + hop) for plane in range(planes - hop)) for hop in range(1, planes)
    ]
    return left + right[1:], tuple(spots)


def stacked(terms, planes):
    return terms.reshape(planes, terms.shape[0] // planes, terms.shape[1])


def scatter_step(planes, step, terms, received, marks=()):
    ups, downs = scatter_cases(planes, step, 0, 1, 2)
    if step == 1:
        ups, downs = ups[:1], downs[:1]
    left, right = mix((ups, downs), (terms, *received), marks)
    received = up(left, 0, step), down(right, planes - 1 - step, planes - 1)
    return received, (left, right)


def exchange_cases(step, terms, outer, inner):
    place = 4 - step
    ends = [(0, 1, [(terms, place)]), (3, 4, [(terms, -place)])]
    if step == 1:
        return ends, []
    inward = [(1, 2, [(terms, place), (outer, None)]), (2, 3, [(terms, -place), (outer, None)])]
    outward = [(1, 2, [(terms, -place), (inner, None)]), (2, 3, [(terms, place), (inner, None)])]
    return ends + outward * (step == 3), inward


def exchange(step, terms, received, marks):
    outer, inner = mix(exchange_cases(step, 0, 1, 2), (terms, *received), marks)
    return (link(outer, *(OUTER if step == 3 else ENDS)), link(inner, *INNER)), (outer, inner)


def whole(planes, first):
    return [
        [(0, planes, first, True)],
        [(0, planes, first + 1, False)],
        [(0, planes, first + 2, False)],
    ]


def local(planes, owners, tokens, q_weight, key_projection, value_projection, q_gain, k_gain, doc_lengths, out_cot):
    groups = key_projection.shape[1] // HEAD_WIDTH
    share = q_weight.shape[1] // key_projection.shape[1]
    wide = share * HEAD_WIDTH
    row_tokens = lax.all_gather(tokens, "seq", axis=0, tiled=True)
    length, model = row_tokens.shape
    rows = length // owners
    tables = doc_tables(doc_lengths[0], length)
    gains = (q_gain[None, :], k_gain[None, :])
    me = lax.axis_index("seq")
    side, pair = lax.rem(me, 2), lax.div(me, 2)

    def halves(group):
        narrow = slice(group * HEAD_WIDTH, (group + 1) * HEAD_WIDTH)
        broad = slice(group * wide, (group + 1) * wide)
        return (
            q_weight[:, broad],
            jnp.concatenate([key_projection[:, narrow], value_projection[:, narrow]], axis=1),
        )

    def group_heads(group, pieces, spots, marks=(), parts=1):
        out, grad, weight, terms = heads(
            share, parts, pieces, spots, row_tokens, tables, gains, doc_lengths,
            out_cot[:, group * wide : (group + 1) * wide], marks,
        )
        return out, grad, weight, stacked(terms, planes)

    def token_part(which, grad, weight, adds=(), parts=(), marks=(), split=False):
        return token_terms(grad, weight, which, owners, adds, parts, marks, split)

    outs, layout, sources = [], [], []
    sent = kept = ()
    paired = groups == 2 and planes == 4
    if paired:
        pieces, spots = gather_four(halves(0))
        block = after(jnp.concatenate(halves(1), axis=1), pieces[4])
        far = link(block, (0, 2), (1, 3), (2, 0), (3, 1))
        block = after(block, pieces[5])
        near, middle = link(block, *OUTER), link(block, *INNER)
        out, grad, weight, terms = group_heads(0, pieces, spots, parts=2)
        outs.append(out)
        (first,) = mix((exchange_cases(1, 0, None, None)[0],), (terms,), ())
        received = (link(first, *ENDS),)
        sent = (token_part(1 - side, grad, weight, marks=(first, far)),)
        last = link(far, *OUTWARD)
        outer_cases, inner_cases = exchange_cases(2, 0, 1, None)
        edges = [(0, 1, [(0, 1)]), (3, 4, [(0, -1)])]
        outer, inner, edge = mix((outer_cases, inner_cases, edges), (terms, *received), (*sent, near, middle))
        received = link(outer, *ENDS), link(inner, *INNER)
        edge_received = link(edge, *ENDS)
        old, early, marks = terms, (grad, weight), (outer, inner, edge)
        pieces = [block, near, middle, far, last]
        spots = (
            tuple((plane, plane) for plane in range(4)),
            tuple((plane, plane ^ 1) for plane in range(4)),
            ((1, 2), (2, 1)),
            tuple((plane, plane ^ 2) for plane in range(4)),
            ((0, 3), (3, 0)),
        )
        out, grad, weight, terms = group_heads(1, pieces, spots, marks)
        outs.append(out)
        outer_cases, inner_cases = exchange_cases(3, 0, 1, 2)
        outer_cases = exchange_cases(1, 3, None, None)[0] + outer_cases[2:]
        marks = mix((outer_cases, inner_cases), (old, *received, terms), ())
        received = link(marks[0], *OUTER), link(marks[1], *INNER)
        layout = [
            [(0, 4, 0, True)],
            [(0, 4, 1, False)],
            [(0, 1, 2, False), (1, 3, 3, False), (3, 4, 2, False)],
        ]
        sources = [old, edge_received, *received]
    else:
        for group in range(groups):
            block = jnp.concatenate(halves(group), axis=1)
            out, grad, weight, terms = group_heads(group, *gather_line(block, planes))
            outs.append(out)
            received, marks = scatter_step(planes, 1, terms, ())
            if group + 1 < groups:
                for step in range(2, planes):
                    received, marks = scatter_step(planes, step, terms, received)
                layout += whole(planes, len(sources))
                sources += [terms, *received]
                sent = (token_part(1 - side, grad, weight, sent),)
                kept = (token_part(side, grad, weight, kept),)
    sent = token_part(1 - side, grad, weight, sent, marks=marks, split=True)
    swapped = [lax.ppermute(part, "seq", [(i, i ^ 1) for i in range(owners)]) for part in sent]
    forward = functools.partial(scatter_step, planes)
    if paired:
        kept = (token_part(side, *early, marks=sent),)
        forward = exchange
    received, marks = forward(2, terms, received[:1] if paired else received, kept)
    kept = token_part(side, grad, weight, kept, swapped, marks)
    shares = [lax.dynamic_index_in_dim(kept, pair, 0, keepdims=False)]
    for other in range(1, owners // 2):
        part = lax.dynamic_index_in_dim(kept, pair ^ other, 0, keepdims=False)
        shares.append(lax.ppermute(part, "seq", [(i, i ^ (2 * other)) for i in range(owners)]))
    marks = (kept,)
    for step in range(3, planes):
        received, marks = forward(step, terms, received, marks)
    spread = lax.all_to_all(
        after(jnp.concatenate(outs, axis=1), *marks),
        "seq",
        split_axis=0,
        concat_axis=0,
        tiled=True,
    )
    layout += whole(planes, len(sources))
    sources += [terms, *received]
    weight_grads = total_terms(share, layout, sources)
    token_grad = add(*shares).astype(jnp.bfloat16)
    attn_out = spread.reshape(owners, rows, groups * wide).transpose(1, 0, 2)
    attn_out = attn_out.reshape(rows, owners * groups * wide)
    return (attn_out, token_grad, *weight_grads)


def solution(mesh):
    rows, split = P(("dp", "seq"), None), P("dp", "seq")
    return jax.shard_map(
        functools.partial(local, mesh.shape["dp"], mesh.shape["seq"]),
        mesh=mesh,
        in_specs=(rows, split, split, split, P(), P(), P("dp", None), split),
        out_specs=(rows, rows, split, split, split),
        check_vma=False,
    )
```

```python
import functools

import jax
import jax.numpy as jnp
from jax import lax
from jax.experimental import pallas as pl
from jax.experimental.pallas import tpu as pltpu
from jax.sharding import PartitionSpec as P

HEAD_WIDTH = 128
WINDOW = 1024
QUERY_BLOCK = 256

score_scale = 168.0 ** (-0.5)
rope_base = 10000.0
log2_e = 1.4426950408889634
norm_eps = 1e-06
NN = (((1,), (0,)), ((), ()))
NT = (((1,), (1,)), ((), ()))
TN = (((0,), (0,)), ((), ()))


def dot(a, b, dims):
    return lax.dot_general(a, b, dims, preferred_element_type=jnp.float32)


def doc_tables(length_row, length):
    ends = jnp.cumsum(length_row, dtype=jnp.int32)
    starts = ends - length_row
    token = jnp.arange(length, dtype=jnp.int32)
    inside = (token[:, None] >= starts[None, :]) & (token[:, None] < ends[None, :])
    start = jnp.sum(jnp.where(inside, starts[None, :], 0), axis=1, dtype=jnp.int32)
    half = HEAD_WIDTH // 2
    inverse = rope_base ** (-jnp.arange(half, dtype=jnp.float32) * (2.0 / HEAD_WIDTH))
    angle = (token - start).astype(jnp.float32)[:, None] * inverse[None, :]
    cosine, sine = jnp.cos(angle), jnp.sin(angle)
    return (
        jnp.concatenate([cosine, cosine], axis=1),
        jnp.concatenate([-sine, sine], axis=1),
    )


def rotate(vectors, gain, cosine, sine):
    factor = lax.rsqrt(jnp.mean(vectors * vectors, axis=1, keepdims=True) + norm_eps)
    normed = vectors * factor * gain
    return normed * cosine + pltpu.roll(normed, HEAD_WIDTH // 2, 1) * sine


def rotate_back(grad, vectors, gain, cosine, sine):
    factor = lax.rsqrt(jnp.mean(vectors * vectors, axis=1, keepdims=True) + norm_eps)
    inner = (grad * cosine + pltpu.roll(grad * sine, HEAD_WIDTH // 2, 1)) * gain
    shared = jnp.mean(inner * vectors, axis=1, keepdims=True) * (factor * factor * factor)
    return inner * factor - vectors * shared


def first_keys(lengths_ref, query_token):
    first, end = jnp.maximum(query_token - (WINDOW - 1), 0), 0
    for document in range(lengths_ref.shape[1]):
        end = end + lengths_ref[0, document]
        first = jnp.maximum(first, jnp.where(query_token >= end, end, 0))
    return first


def head_kernel(share, halves, spots, marks, lengths_ref, qgain_ref, kgain_ref, *refs):
    count = len(spots)
    pieces = refs[:count]
    tokens_hbm, cos_hbm, sin_hbm, cot_hbm = refs[count : count + 4]
    refs = refs[count + 4 + marks :]
    out_ref, grad_ref, weight_hbm, terms_hbm = refs[:4]
    (tok, weight, cos_ref, sin_ref, cot_ref, proj, query, key, value, key_sum, value_sum, terms) = refs[4:16]
    piece_sem, tok_sem, small_sem, weight_sem, terms_sem = refs[16:]
    length, rows = tok.shape[0], pieces[0].shape[0]
    part_width = weight.shape[1] // halves
    blocks = length // QUERY_BLOCK
    mine = lax.axis_index("dp")

    def each_piece(act):
        for index, planes in enumerate(spots):
            half = index * halves // count
            cols = pl.ds(half * part_width, part_width)
            place = functools.reduce(
                lambda other, spot: jnp.where(mine == spot[0], spot[1], other), planes, 0
            )
            here = functools.reduce(
                lambda other, spot: other | (mine == spot[0]), planes[1:], mine == planes[0][0]
            )

            @pl.when(here)
            def _():
                at = pl.ds(pl.multiple_of(place * rows, 16), rows)
                act(pltpu.make_async_copy(pieces[index], weight.at[at, cols], piece_sem.at[index]))

    def tok_copy(block):
        at = pl.ds(pl.multiple_of(block * QUERY_BLOCK, QUERY_BLOCK), QUERY_BLOCK)
        return pltpu.make_async_copy(tokens_hbm.at[at], tok.at[at], tok_sem.at[block])

    small = [
        pltpu.make_async_copy(source, target, small_sem.at[slot])
        for slot, (source, target) in enumerate(
            ((cos_hbm, cos_ref), (sin_hbm, sin_ref), (cot_hbm, cot_ref))
        )
    ]
    each_piece(lambda copy: copy.start())
    for block in range(blocks):
        tok_copy(block).start()
    for copy in small:
        copy.start()
    each_piece(lambda copy: copy.wait())
    weight_copy = pltpu.make_async_copy(weight, weight_hbm, weight_sem)
    weight_copy.start()

    qgain, kgain = qgain_ref[...], kgain_ref[...]
    key_at, value_at = share * HEAD_WIDTH, (share + 1) * HEAD_WIDTH
    for copy in small:
        copy.wait()

    @pl.loop(0, blocks)
    def _(block):
        tok_copy(block).wait()
        at = pl.ds(pl.multiple_of(block * QUERY_BLOCK, QUERY_BLOCK), QUERY_BLOCK)
        part = dot(tok[at, :], weight[...], NN)
        proj[at, :] = part
        cosine, sine = cos_ref[at, :], sin_ref[at, :]
        for head in range(share):
            cols = slice(head * HEAD_WIDTH, (head + 1) * HEAD_WIDTH)
            query[at, cols] = rotate(part[:, cols], qgain, cosine, sine).astype(jnp.bfloat16)
        key[at, :] = rotate(part[:, key_at:value_at], kgain, cosine, sine).astype(jnp.bfloat16)
        value[at, :] = part[:, value_at:].astype(jnp.bfloat16)

    key_sum[...] = jnp.zeros_like(key_sum)
    value_sum[...] = jnp.zeros_like(value_sum)
    for block in range(blocks):
        start = block * QUERY_BLOCK
        low = max(0, (start - (WINDOW - 1)) // QUERY_BLOCK * QUERY_BLOCK)
        width = start + QUERY_BLOCK - low
        at, keys_at = pl.ds(start, QUERY_BLOCK), pl.ds(low, width)
        key_token = low + lax.broadcasted_iota(jnp.int32, (QUERY_BLOCK, width), 1)
        query_token = start + lax.broadcasted_iota(jnp.int32, (QUERY_BLOCK, 1), 0)
        allowed = (key_token >= first_keys(lengths_ref, query_token)) & (key_token <= query_token)
        key_part, value_part = key[keys_at, :], value[keys_at, :]
        cosine, sine = cos_ref[at, :], sin_ref[at, :]
        for head in range(share):
            cols = slice(head * HEAD_WIDTH, (head + 1) * HEAD_WIDTH)
            query_part, cot_part = query[at, cols], cot_ref[at, cols]
            scores = dot(query_part, key_part, NT) * (score_scale * log2_e)
            weights = jnp.where(allowed, jnp.exp2(scores), 0.0)
            probs = weights * (1.0 / jnp.sum(weights, axis=1, keepdims=True))
            probs_bf = probs.astype(jnp.bfloat16)
            mixed = dot(probs_bf, value_part, NN)
            out_ref[at, cols] = mixed.astype(jnp.bfloat16)
            value_sum[keys_at, :] += dot(probs_bf, cot_part, TN)
            grad_probs = dot(cot_part, value_part, NT)
            delta = jnp.sum(mixed * cot_part.astype(jnp.float32), axis=1, keepdims=True)
            grad_scores = (probs * (grad_probs - delta)).astype(jnp.bfloat16)
            key_sum[keys_at, :] += dot(grad_scores, query_part, TN)
            grad_query = dot(grad_scores, key_part, NN) * score_scale
            grad_ref[at, cols] = rotate_back(
                grad_query, proj[at, cols], qgain, cosine, sine
            ).astype(jnp.bfloat16)
    for block in range(blocks):
        at = pl.ds(block * QUERY_BLOCK, QUERY_BLOCK)
        grad_ref[at, key_at:value_at] = rotate_back(
            key_sum[at, :] * score_scale,
            proj[at, key_at:value_at],
            kgain,
            cos_ref[at, :],
            sin_ref[at, :],
        ).astype(jnp.bfloat16)
        grad_ref[at, value_at:] = value_sum[at, :].astype(jnp.bfloat16)

    grads = grad_ref[...]
    model = tok.shape[1]
    depth = model // terms_sem.shape[0]

    def terms_copy(part):
        at = pl.ds(pl.multiple_of(part * depth, HEAD_WIDTH), depth)
        return pltpu.make_async_copy(terms.at[at], terms_hbm.at[at], terms_sem.at[part])

    @pl.loop(0, terms_sem.shape[0])
    def _(part):
        at = pl.ds(pl.multiple_of(part * depth, HEAD_WIDTH), depth)
        terms[at, :] = dot(tok[:, at], grads, TN).astype(jnp.bfloat16)
        terms_copy(part).start()

    @pl.loop(0, terms_sem.shape[0])
    def _(part):
        terms_copy(part).wait()

    weight_copy.wait()


def heads(share, halves, pieces, spots, row_tokens, tables, gains, lengths, cot, marks):
    length, model = row_tokens.shape
    width = pieces[0].shape[1] * halves
    blocks = length // QUERY_BLOCK
    parts = max(k for k in (1, 3, 7) if model % (k * HEAD_WIDTH) == 0)
    hbm = pl.BlockSpec(memory_space=pltpu.HBM)
    vmem = pl.BlockSpec(memory_space=pltpu.VMEM)
    table = pltpu.VMEM((length, HEAD_WIDTH), jnp.float32)
    return pl.pallas_call(
        functools.partial(head_kernel, share, halves, spots, len(marks)),
        out_shape=(
            jax.ShapeDtypeStruct((length, share * HEAD_WIDTH), jnp.bfloat16),
            jax.ShapeDtypeStruct((length, width), jnp.bfloat16),
            jax.ShapeDtypeStruct((model, width), jnp.bfloat16),
            jax.ShapeDtypeStruct((model, width), jnp.bfloat16),
        ),
        in_specs=[pl.BlockSpec(memory_space=pltpu.SMEM), vmem, vmem]
        + [hbm] * (len(pieces) + 4 + len(marks)),
        out_specs=(vmem, vmem, hbm, hbm),
        scratch_shapes=[
            pltpu.VMEM((length, model), jnp.bfloat16),
            pltpu.VMEM((model, width), jnp.bfloat16),
            table,
            table,
            pltpu.VMEM((length, share * HEAD_WIDTH), jnp.bfloat16),
            pltpu.VMEM((length, width), jnp.float32),
            pltpu.VMEM((length, share * HEAD_WIDTH), jnp.bfloat16),
            pltpu.VMEM((length, HEAD_WIDTH), jnp.bfloat16),
            pltpu.VMEM((length, HEAD_WIDTH), jnp.bfloat16),
            table,
            table,
            pltpu.VMEM((model, width), jnp.bfloat16),
            pltpu.SemaphoreType.DMA((len(pieces),)),
            pltpu.SemaphoreType.DMA((blocks,)),
            pltpu.SemaphoreType.DMA((3,)),
            pltpu.SemaphoreType.DMA,
            pltpu.SemaphoreType.DMA((parts,)),
        ],
        compiler_params=pltpu.CompilerParams(vmem_limit_bytes=65024 * 1024),
        cost_estimate=pl.CostEstimate(
            flops=4 * length * model * width + 12 * share * length * length * HEAD_WIDTH,
            bytes_accessed=2 * (length * model + 3 * model * width + 4 * length * width),
            transcendentals=share * length * length,
        ),
        name="heads",
    )(lengths, *gains, *pieces, row_tokens, *tables, cot, *marks)


def token_kernel(adds, parts, marks, side_ref, grad_ref, weight_ref, *refs):
    grad = grad_ref[...]
    batch, rows = grad.shape[:2]
    grad = grad.reshape(batch * rows, grad.shape[2])
    total = dot(grad, weight_ref[...], NT).reshape(batch, rows, weight_ref.shape[0])
    for index in range(adds):
        total = total + refs[index][...].astype(jnp.float32)
    pieces, outs = refs[adds : adds + parts], refs[adds + parts + marks :]
    if not parts and len(outs) == 1:
        outs[0][...] = total.astype(jnp.bfloat16)
        return
    count = parts or len(outs)
    for place in range(count):

        @pl.when(pl.program_id(0) == place // batch)
        def _():
            row = total[place % batch]
            if parts:
                row = row + pieces[place][...].astype(jnp.float32)
                outs[0][place % batch] = row.astype(jnp.bfloat16)
            else:
                outs[place][...] = row.astype(jnp.bfloat16)


def token_terms(grad, weight, side, owners, adds, parts, marks, split):
    length, width = grad.shape
    model = weight.shape[0]
    rows, pairs = length // owners, owners // 2
    batch = 2 if pairs % 2 == 0 else 1
    block = pl.BlockSpec((batch, rows, model), lambda i, side_ref: (i, 0, 0))
    single = pl.BlockSpec((rows, model), lambda i, side_ref: (0, 0))
    out_specs, out_shape = block, jax.ShapeDtypeStruct((pairs, rows, model), jnp.bfloat16)
    if split:
        out_specs = (single,) * pairs
        out_shape = (jax.ShapeDtypeStruct((rows, model), jnp.bfloat16),) * pairs
    return pl.pallas_call(
        functools.partial(token_kernel, len(adds), len(parts), len(marks)),
        grid_spec=pltpu.PrefetchScalarGridSpec(
            num_scalar_prefetch=1,
            grid=(pairs // batch,),
            in_specs=[
                pl.BlockSpec(
                    (batch, None, rows, width), lambda i, side_ref: (i, side_ref[0], 0, 0)
                ),
                pl.BlockSpec((model, width), lambda i, side_ref: (0, 0)),
            ]
            + [block] * len(adds)
            + [single] * len(parts)
            + [pl.BlockSpec(memory_space=pltpu.HBM)] * len(marks),
            out_specs=out_specs,
        ),
        out_shape=out_shape,
        compiler_params=pltpu.CompilerParams(vmem_limit_bytes=65024 * 1024),
        cost_estimate=pl.CostEstimate(
            flops=length * width, bytes_accessed=length * width, transcendentals=0
        ),
        name="token_terms",
    )(side.reshape(1), grad.reshape(pairs, 2, rows, width), weight, *adds, *parts, *marks)


def mix_kernel(outs, count, marks, *refs):
    sources, refs = refs[:count], refs[count + marks :]
    targets, extra, sem = refs[: len(outs)], refs[len(outs) : -1], refs[-1]
    mine = lax.axis_index("dp")

    def each(act):
        for index, cases in enumerate(outs):
            for low, high, terms in cases:
                copies = []

                @pl.when((mine >= low) & (mine < high))
                def _():
                    for slot, (source, place) in enumerate(terms):
                        ref = sources[source]
                        ref = ref if place is None else ref.at[mine + place]
                        target = targets[index] if slot == 0 else extra[index]
                        copies.append(pltpu.make_async_copy(ref, target, sem.at[index, slot]))
                    act(index, copies)

    def start(index, copies):
        for copy in copies:
            copy.start()

    def finish(index, copies):
        for copy in copies:
            copy.wait()
        if len(copies) > 1:
            total = targets[index][...].astype(jnp.float32) + extra[index][...].astype(jnp.float32)
            targets[index][...] = total.astype(jnp.bfloat16)

    each(start)
    each(finish)


def mix(outs, sources, marks):
    shape = sources[0].shape[-2:]
    plain = pl.BlockSpec(memory_space=pl.ANY)
    vmem = pl.BlockSpec(memory_space=pltpu.VMEM)
    return pl.pallas_call(
        functools.partial(mix_kernel, outs, len(sources), len(marks)),
        out_shape=(jax.ShapeDtypeStruct(shape, jnp.bfloat16),) * len(outs),
        in_specs=[plain] * (len(sources) + len(marks)),
        out_specs=(vmem,) * len(outs),
        scratch_shapes=[pltpu.VMEM(shape, jnp.bfloat16)] * len(outs)
        + [pltpu.SemaphoreType.DMA((len(outs), 2))],
        compiler_params=pltpu.CompilerParams(vmem_limit_bytes=65024 * 1024),
        cost_estimate=pl.CostEstimate(flops=1, bytes_accessed=1, transcendentals=0),
        name="mix",
    )(*sources, *marks)


def scatter_cases(planes, step, terms, received_up, received_down):
    first, last = planes - step, step - planes
    ups = [(0, 1, [(terms, first)]), (1, step, [(terms, first), (received_up, None)])]
    downs = [
        (planes - 1, planes, [(terms, last)]),
        (planes - step, planes - 1, [(terms, last), (received_down, None)]),
    ]
    return ups, downs


def total_kernel(share, layout, count, *refs):
    sources, outs, pieces, sem = refs[:count], refs[count : count + 3], refs[count + 3 : -1], refs[-1]
    mine = lax.axis_index("dp")

    def each(act):
        for index, cases in enumerate(layout):
            for low, high, source, own in cases:

                @pl.when((mine >= low) & (mine < high))
                def _():
                    ref = sources[source].at[mine] if own else sources[source]
                    act(pltpu.make_async_copy(ref, pieces[index], sem.at[index]))

    each(lambda copy: copy.start())
    each(lambda copy: copy.wait())
    wide = share * HEAD_WIDTH
    for group in range(len(layout) // 3):
        total = sum(pieces[3 * group + index][...].astype(jnp.float32) for index in range(3))
        outs[0][:, group * wide : (group + 1) * wide] = total[:, :wide]
        narrow = slice(group * HEAD_WIDTH, (group + 1) * HEAD_WIDTH)
        outs[1][:, narrow] = total[:, wide : wide + HEAD_WIDTH]
        outs[2][:, narrow] = total[:, wide + HEAD_WIDTH :]


def total_terms(share, layout, sources):
    groups = len(layout) // 3
    rows, width = sources[0].shape[-2:]
    plain = pl.BlockSpec(memory_space=pl.ANY)
    vmem = pl.BlockSpec(memory_space=pltpu.VMEM)
    return pl.pallas_call(
        functools.partial(total_kernel, share, layout, len(sources)),
        out_shape=tuple(
            jax.ShapeDtypeStruct((rows, groups * count * HEAD_WIDTH), jnp.float32)
            for count in (share, 1, 1)
        ),
        in_specs=[plain] * len(sources),
        out_specs=(vmem,) * 3,
        scratch_shapes=[pltpu.VMEM((rows, width), jnp.bfloat16)] * len(layout)
        + [pltpu.SemaphoreType.DMA((len(layout),))],
        compiler_params=pltpu.CompilerParams(vmem_limit_bytes=65024 * 1024),
        cost_estimate=pl.CostEstimate(flops=1, bytes_accessed=1, transcendentals=0),
        name="total_terms",
    )(*sources)


def after(value, *others):
    return lax.optimization_barrier((value, *others))[0]


def up(value, first, last):
    return lax.ppermute(value, "dp", [(i, i + 1) for i in range(first, last)])


def down(value, first, last):
    return lax.ppermute(value, "dp", [(i + 1, i) for i in range(first, last)])


def add(*terms):
    return functools.reduce(lambda a, b: a + b, [term.astype(jnp.float32) for term in terms])


def link(value, *pairs):
    return lax.ppermute(value, "dp", pairs)


ENDS = ((0, 1), (3, 2))
OUTER = ((0, 1), (1, 0), (2, 3), (3, 2))
INNER = ((1, 2), (2, 1))
OUTWARD = ((1, 0), (2, 3))


def gather_four(parts):
    outer = [link(part, *OUTER) for part in parts]
    inner = [link(part, *INNER) for part in parts]
    inner_second = [link(part, *INNER) for part in outer]
    outer_second = [link(part, *OUTWARD) for part in inner]
    outer_third = [link(part, *OUTWARD) for part in inner_second]
    own = tuple((plane, plane) for plane in range(4))
    swap = tuple((plane, plane ^ 1) for plane in range(4))
    spots = (own, swap, ((1, 2), (2, 1)), ((1, 3), (2, 0)), ((0, 2), (3, 1)), ((0, 3), (3, 0)))
    columns = zip(parts, outer, inner, inner_second, outer_second, outer_third)
    return [piece for column in columns for piece in column], spots * len(parts)


def gather_line(block, planes):
    left, right = [block], [block]
    for step in range(planes - 1):
        left.append(up(left[-1], step, planes - 1))
        right.append(down(right[-1], 0, planes - 1 - step))
    spots = [tuple((plane, plane - hop) for plane in range(hop, planes)) for hop in range(planes)]
    spots += [
        tuple((plane, plane + hop) for plane in range(planes - hop)) for hop in range(1, planes)
    ]
    return left + right[1:], tuple(spots)


def stacked(terms, planes):
    return terms.reshape(planes, terms.shape[0] // planes, terms.shape[1])


def scatter_step(planes, step, terms, received, marks=()):
    ups, downs = scatter_cases(planes, step, 0, 1, 2)
    if step == 1:
        ups, downs = ups[:1], downs[:1]
    left, right = mix((ups, downs), (terms, *received), marks)
    received = up(left, 0, step), down(right, planes - 1 - step, planes - 1)
    return received, (left, right)


def exchange_cases(step, terms, outer, inner):
    place = 4 - step
    ends = [(0, 1, [(terms, place)]), (3, 4, [(terms, -place)])]
    if step == 1:
        return ends, []
    inward = [(1, 2, [(terms, place), (outer, None)]), (2, 3, [(terms, -place), (outer, None)])]
    outward = [(1, 2, [(terms, -place), (inner, None)]), (2, 3, [(terms, place), (inner, None)])]
    return ends + outward * (step == 3), inward


def exchange(step, terms, received, marks):
    outer, inner = mix(exchange_cases(step, 0, 1, 2), (terms, *received), marks)
    return (link(outer, *(OUTER if step == 3 else ENDS)), link(inner, *INNER)), (outer, inner)


def whole(planes, first):
    return [
        [(0, planes, first, True)],
        [(0, planes, first + 1, False)],
        [(0, planes, first + 2, False)],
    ]


def local(planes, owners, tokens, q_weight, key_projection, value_projection, q_gain, k_gain, doc_lengths, out_cot):
    groups = key_projection.shape[1] // HEAD_WIDTH
    share = q_weight.shape[1] // key_projection.shape[1]
    wide = share * HEAD_WIDTH
    row_tokens = lax.all_gather(tokens, "seq", axis=0, tiled=True)
    length, model = row_tokens.shape
    rows = length // owners
    tables = doc_tables(doc_lengths[0], length)
    gains = (q_gain[None, :], k_gain[None, :])
    me = lax.axis_index("seq")
    side, pair = lax.rem(me, 2), lax.div(me, 2)

    def halves(group):
        narrow = slice(group * HEAD_WIDTH, (group + 1) * HEAD_WIDTH)
        broad = slice(group * wide, (group + 1) * wide)
        return (
            q_weight[:, broad],
            jnp.concatenate([key_projection[:, narrow], value_projection[:, narrow]], axis=1),
        )

    def group_heads(group, pieces, spots, marks=(), parts=1):
        out, grad, weight, terms = heads(
            share, parts, pieces, spots, row_tokens, tables, gains, doc_lengths,
            out_cot[:, group * wide : (group + 1) * wide], marks,
        )
        return out, grad, weight, stacked(terms, planes)

    def token_part(which, grad, weight, adds=(), parts=(), marks=(), split=False):
        return token_terms(grad, weight, which, owners, adds, parts, marks, split)

    outs, layout, sources = [], [], []
    sent = kept = ()
    paired = groups == 2 and planes == 4
    if paired:
        pieces, spots = gather_four(halves(0))
        block = after(jnp.concatenate(halves(1), axis=1), pieces[4])
        far = link(block, (0, 2), (1, 3), (2, 0), (3, 1))
        block = after(block, pieces[5])
        near, middle = link(block, *OUTER), link(block, *INNER)
        out, grad, weight, terms = group_heads(0, pieces, spots, parts=2)
        outs.append(out)
        (first,) = mix((exchange_cases(1, 0, None, None)[0],), (terms,), ())
        received = (link(first, *ENDS),)
        sent = (token_part(1 - side, grad, weight, marks=(first, far)),)
        last = link(far, *OUTWARD)
        outer_cases, inner_cases = exchange_cases(2, 0, 1, None)
        edges = [(0, 1, [(0, 1)]), (3, 4, [(0, -1)])]
        outer, inner, edge = mix((outer_cases, inner_cases, edges), (terms, *received), (*sent, near, middle))
        received = link(outer, *ENDS), link(inner, *INNER)
        edge_received = link(edge, *ENDS)
        old, early, marks = terms, (grad, weight), (outer, inner, edge)
        pieces = [block, near, middle, far, last]
        spots = (
            tuple((plane, plane) for plane in range(4)),
            tuple((plane, plane ^ 1) for plane in range(4)),
            ((1, 2), (2, 1)),
            tuple((plane, plane ^ 2) for plane in range(4)),
            ((0, 3), (3, 0)),
        )
        out, grad, weight, terms = group_heads(1, pieces, spots, marks)
        outs.append(out)
        outer_cases, inner_cases = exchange_cases(3, 0, 1, 2)
        outer_cases = exchange_cases(1, 3, None, None)[0] + outer_cases[2:]
        marks = mix((outer_cases, inner_cases), (old, *received, terms), (edge_received,))
        received = link(marks[0], *OUTER), link(marks[1], *INNER)
        layout = [
            [(0, 4, 0, True)],
            [(0, 4, 1, False)],
            [(0, 1, 2, False), (1, 3, 3, False), (3, 4, 2, False)],
        ]
        sources = [old, edge_received, *received]
    else:
        for group in range(groups):
            block = jnp.concatenate(halves(group), axis=1)
            out, grad, weight, terms = group_heads(group, *gather_line(block, planes))
            outs.append(out)
            received, marks = scatter_step(planes, 1, terms, ())
            if group + 1 < groups:
                for step in range(2, planes):
                    received, marks = scatter_step(planes, step, terms, received)
                layout += whole(planes, len(sources))
                sources += [terms, *received]
                sent = (token_part(1 - side, grad, weight, sent),)
                kept = (token_part(side, grad, weight, kept),)
    sent = token_part(1 - side, grad, weight, sent, marks=marks, split=True)
    swapped = [lax.ppermute(part, "seq", [(i, i ^ 1) for i in range(owners)]) for part in sent]
    forward = functools.partial(scatter_step, planes)
    if paired:
        kept = (token_part(side, *early, marks=sent),)
        forward = exchange
    received, marks = forward(2, terms, received[:1] if paired else received, kept)
    kept = token_part(side, grad, weight, kept, swapped, marks)
    shares = [lax.dynamic_index_in_dim(kept, pair, 0, keepdims=False)]
    for other in range(1, owners // 2):
        part = lax.dynamic_index_in_dim(kept, pair ^ other, 0, keepdims=False)
        shares.append(lax.ppermute(part, "seq", [(i, i ^ (2 * other)) for i in range(owners)]))
    marks = (kept,)
    for step in range(3, planes):
        received, marks = forward(step, terms, received, marks)
    spread = lax.all_to_all(
        after(jnp.concatenate(outs, axis=1), *marks),
        "seq",
        split_axis=0,
        concat_axis=0,
        tiled=True,
    )
    layout += whole(planes, len(sources))
    sources += [terms, *received]
    attn_out = spread.reshape(owners, rows, groups * wide).transpose(1, 0, 2)
    attn_out = attn_out.reshape(rows, owners * groups * wide)
    sources[0] = after(sources[0], attn_out)
    weight_grads = total_terms(share, layout, sources)
    token_grad = add(*shares).astype(jnp.bfloat16)
    return (attn_out, token_grad, *weight_grads)


def solution(mesh):
    rows, split = P(("dp", "seq"), None), P("dp", "seq")
    return jax.shard_map(
        functools.partial(local, mesh.shape["dp"], mesh.shape["seq"]),
        mesh=mesh,
        in_specs=(rows, split, split, split, P(), P(), P("dp", None), split),
        out_specs=(rows, rows, split, split, split),
        check_vma=False,
    )
```

```python
import functools

import jax
import jax.numpy as jnp
from jax import lax
from jax.experimental import pallas as pl
from jax.experimental.pallas import tpu as pltpu
from jax.sharding import PartitionSpec as P

HEAD_WIDTH = 128
WINDOW = 1024
QUERY_BLOCK = 256

score_scale = 168.0 ** (-0.5)
rope_base = 10000.0
log2_e = 1.4426950408889634
norm_eps = 1e-06
NN = (((1,), (0,)), ((), ()))
NT = (((1,), (1,)), ((), ()))
TN = (((0,), (0,)), ((), ()))


def dot(a, b, dims):
    return lax.dot_general(a, b, dims, preferred_element_type=jnp.float32)


def doc_tables(length_row, length):
    ends = jnp.cumsum(length_row, dtype=jnp.int32)
    starts = ends - length_row
    token = jnp.arange(length, dtype=jnp.int32)
    inside = (token[:, None] >= starts[None, :]) & (token[:, None] < ends[None, :])
    start = jnp.sum(jnp.where(inside, starts[None, :], 0), axis=1, dtype=jnp.int32)
    half = HEAD_WIDTH // 2
    inverse = rope_base ** (-jnp.arange(half, dtype=jnp.float32) * (2.0 / HEAD_WIDTH))
    angle = (token - start).astype(jnp.float32)[:, None] * inverse[None, :]
    cosine, sine = jnp.cos(angle), jnp.sin(angle)
    return (
        jnp.concatenate([cosine, cosine], axis=1),
        jnp.concatenate([-sine, sine], axis=1),
    )


def rotate(vectors, gain, cosine, sine):
    factor = lax.rsqrt(jnp.mean(vectors * vectors, axis=1, keepdims=True) + norm_eps)
    normed = vectors * factor * gain
    return normed * cosine + pltpu.roll(normed, HEAD_WIDTH // 2, 1) * sine


def rotate_back(grad, vectors, gain, cosine, sine):
    factor = lax.rsqrt(jnp.mean(vectors * vectors, axis=1, keepdims=True) + norm_eps)
    inner = (grad * cosine + pltpu.roll(grad * sine, HEAD_WIDTH // 2, 1)) * gain
    shared = jnp.mean(inner * vectors, axis=1, keepdims=True) * (factor * factor * factor)
    return inner * factor - vectors * shared


def first_keys(lengths_ref, query_token):
    first, end = jnp.maximum(query_token - (WINDOW - 1), 0), 0
    for document in range(lengths_ref.shape[1]):
        end = end + lengths_ref[0, document]
        first = jnp.maximum(first, jnp.where(query_token >= end, end, 0))
    return first


def head_kernel(share, halves, spots, marks, lengths_ref, qgain_ref, kgain_ref, *refs):
    count = len(spots)
    pieces = refs[:count]
    tokens_hbm, cos_hbm, sin_hbm, cot_hbm = refs[count : count + 4]
    refs = refs[count + 4 + marks :]
    out_ref, grad_ref, weight_hbm, terms_hbm = refs[:4]
    (tok, weight, cos_ref, sin_ref, cot_ref, proj, query, key, value, key_sum, value_sum, terms) = refs[4:16]
    piece_sem, tok_sem, small_sem, weight_sem, terms_sem = refs[16:]
    length, rows = tok.shape[0], pieces[0].shape[0]
    part_width = weight.shape[1] // halves
    blocks = length // QUERY_BLOCK
    mine = lax.axis_index("dp")

    def each_piece(act):
        for index, planes in enumerate(spots):
            half = index * halves // count
            cols = pl.ds(half * part_width, part_width)
            place = functools.reduce(
                lambda other, spot: jnp.where(mine == spot[0], spot[1], other), planes, 0
            )
            here = functools.reduce(
                lambda other, spot: other | (mine == spot[0]), planes[1:], mine == planes[0][0]
            )

            @pl.when(here)
            def _():
                at = pl.ds(pl.multiple_of(place * rows, 16), rows)
                act(pltpu.make_async_copy(pieces[index], weight.at[at, cols], piece_sem.at[index]))

    def tok_copy(block):
        at = pl.ds(pl.multiple_of(block * QUERY_BLOCK, QUERY_BLOCK), QUERY_BLOCK)
        return pltpu.make_async_copy(tokens_hbm.at[at], tok.at[at], tok_sem.at[block])

    small = [
        pltpu.make_async_copy(source, target, small_sem.at[slot])
        for slot, (source, target) in enumerate(
            ((cos_hbm, cos_ref), (sin_hbm, sin_ref), (cot_hbm, cot_ref))
        )
    ]
    each_piece(lambda copy: copy.start())
    for block in range(blocks):
        tok_copy(block).start()
    for copy in small:
        copy.start()
    each_piece(lambda copy: copy.wait())
    weight_copy = pltpu.make_async_copy(weight, weight_hbm, weight_sem)
    weight_copy.start()

    qgain, kgain = qgain_ref[...], kgain_ref[...]
    key_at, value_at = share * HEAD_WIDTH, (share + 1) * HEAD_WIDTH
    for copy in small:
        copy.wait()

    @pl.loop(0, blocks)
    def _(block):
        tok_copy(block).wait()
        at = pl.ds(pl.multiple_of(block * QUERY_BLOCK, QUERY_BLOCK), QUERY_BLOCK)
        part = dot(tok[at, :], weight[...], NN)
        proj[at, :] = part
        cosine, sine = cos_ref[at, :], sin_ref[at, :]
        for head in range(share):
            cols = slice(head * HEAD_WIDTH, (head + 1) * HEAD_WIDTH)
            query[at, cols] = rotate(part[:, cols], qgain, cosine, sine).astype(jnp.bfloat16)
        key[at, :] = rotate(part[:, key_at:value_at], kgain, cosine, sine).astype(jnp.bfloat16)
        value[at, :] = part[:, value_at:].astype(jnp.bfloat16)

    key_sum[...] = jnp.zeros_like(key_sum)
    value_sum[...] = jnp.zeros_like(value_sum)
    for block in range(blocks):
        start = block * QUERY_BLOCK
        low = max(0, (start - (WINDOW - 1)) // QUERY_BLOCK * QUERY_BLOCK)
        width = start + QUERY_BLOCK - low
        at, keys_at = pl.ds(start, QUERY_BLOCK), pl.ds(low, width)
        key_token = low + lax.broadcasted_iota(jnp.int32, (QUERY_BLOCK, width), 1)
        query_token = start + lax.broadcasted_iota(jnp.int32, (QUERY_BLOCK, 1), 0)
        allowed = (key_token >= first_keys(lengths_ref, query_token)) & (key_token <= query_token)
        key_part, value_part = key[keys_at, :], value[keys_at, :]
        cosine, sine = cos_ref[at, :], sin_ref[at, :]
        for head in range(share):
            cols = slice(head * HEAD_WIDTH, (head + 1) * HEAD_WIDTH)
            query_part, cot_part = query[at, cols], cot_ref[at, cols]
            scores = dot(query_part, key_part, NT) * (score_scale * log2_e)
            weights = jnp.where(allowed, jnp.exp2(scores), 0.0)
            probs = weights * (1.0 / jnp.sum(weights, axis=1, keepdims=True))
            probs_bf = probs.astype(jnp.bfloat16)
            mixed = dot(probs_bf, value_part, NN)
            out_ref[at, cols] = mixed.astype(jnp.bfloat16)
            value_sum[keys_at, :] += dot(probs_bf, cot_part, TN)
            grad_probs = dot(cot_part, value_part, NT)
            delta = jnp.sum(mixed * cot_part.astype(jnp.float32), axis=1, keepdims=True)
            grad_scores = (probs * (grad_probs - delta)).astype(jnp.bfloat16)
            key_sum[keys_at, :] += dot(grad_scores, query_part, TN)
            grad_query = dot(grad_scores, key_part, NN) * score_scale
            grad_ref[at, cols] = rotate_back(
                grad_query, proj[at, cols], qgain, cosine, sine
            ).astype(jnp.bfloat16)
    for block in range(blocks):
        at = pl.ds(block * QUERY_BLOCK, QUERY_BLOCK)
        grad_ref[at, key_at:value_at] = rotate_back(
            key_sum[at, :] * score_scale,
            proj[at, key_at:value_at],
            kgain,
            cos_ref[at, :],
            sin_ref[at, :],
        ).astype(jnp.bfloat16)
        grad_ref[at, value_at:] = value_sum[at, :].astype(jnp.bfloat16)

    grads = grad_ref[...]
    model = tok.shape[1]
    depth = model // terms_sem.shape[0]

    def terms_copy(part):
        at = pl.ds(pl.multiple_of(part * depth, HEAD_WIDTH), depth)
        return pltpu.make_async_copy(terms.at[at], terms_hbm.at[at], terms_sem.at[part])

    @pl.loop(0, terms_sem.shape[0])
    def _(part):
        at = pl.ds(pl.multiple_of(part * depth, HEAD_WIDTH), depth)
        terms[at, :] = dot(tok[:, at], grads, TN).astype(jnp.bfloat16)
        terms_copy(part).start()

    @pl.loop(0, terms_sem.shape[0])
    def _(part):
        terms_copy(part).wait()

    weight_copy.wait()


def heads(share, halves, pieces, spots, row_tokens, tables, gains, lengths, cot, marks):
    length, model = row_tokens.shape
    width = pieces[0].shape[1] * halves
    blocks = length // QUERY_BLOCK
    parts = max(k for k in (1, 3, 7) if model % (k * HEAD_WIDTH) == 0)
    hbm = pl.BlockSpec(memory_space=pltpu.HBM)
    vmem = pl.BlockSpec(memory_space=pltpu.VMEM)
    table = pltpu.VMEM((length, HEAD_WIDTH), jnp.float32)
    return pl.pallas_call(
        functools.partial(head_kernel, share, halves, spots, len(marks)),
        out_shape=(
            jax.ShapeDtypeStruct((length, share * HEAD_WIDTH), jnp.bfloat16),
            jax.ShapeDtypeStruct((length, width), jnp.bfloat16),
            jax.ShapeDtypeStruct((model, width), jnp.bfloat16),
            jax.ShapeDtypeStruct((model, width), jnp.bfloat16),
        ),
        in_specs=[pl.BlockSpec(memory_space=pltpu.SMEM), vmem, vmem]
        + [hbm] * (len(pieces) + 4 + len(marks)),
        out_specs=(vmem, vmem, hbm, hbm),
        scratch_shapes=[
            pltpu.VMEM((length, model), jnp.bfloat16),
            pltpu.VMEM((model, width), jnp.bfloat16),
            table,
            table,
            pltpu.VMEM((length, share * HEAD_WIDTH), jnp.bfloat16),
            pltpu.VMEM((length, width), jnp.float32),
            pltpu.VMEM((length, share * HEAD_WIDTH), jnp.bfloat16),
            pltpu.VMEM((length, HEAD_WIDTH), jnp.bfloat16),
            pltpu.VMEM((length, HEAD_WIDTH), jnp.bfloat16),
            table,
            table,
            pltpu.VMEM((model, width), jnp.bfloat16),
            pltpu.SemaphoreType.DMA((len(pieces),)),
            pltpu.SemaphoreType.DMA((blocks,)),
            pltpu.SemaphoreType.DMA((3,)),
            pltpu.SemaphoreType.DMA,
            pltpu.SemaphoreType.DMA((parts,)),
        ],
        compiler_params=pltpu.CompilerParams(vmem_limit_bytes=65024 * 1024),
        cost_estimate=pl.CostEstimate(
            flops=4 * length * model * width + 12 * share * length * length * HEAD_WIDTH,
            bytes_accessed=2 * (length * model + 3 * model * width + 4 * length * width),
            transcendentals=share * length * length,
        ),
        name="heads",
    )(lengths, *gains, *pieces, row_tokens, *tables, cot, *marks)


def token_kernel(adds, parts, marks, side_ref, grad_ref, weight_ref, *refs):
    grad = grad_ref[...]
    batch, rows = grad.shape[:2]
    grad = grad.reshape(batch * rows, grad.shape[2])
    total = dot(grad, weight_ref[...], NT).reshape(batch, rows, weight_ref.shape[0])
    for index in range(adds):
        total = total + refs[index][...].astype(jnp.float32)
    pieces, outs = refs[adds : adds + parts], refs[adds + parts + marks :]
    if not parts and len(outs) == 1:
        outs[0][...] = total.astype(jnp.bfloat16)
        return
    count = parts or len(outs)
    for place in range(count):

        @pl.when(pl.program_id(0) == place // batch)
        def _():
            row = total[place % batch]
            if parts:
                row = row + pieces[place][...].astype(jnp.float32)
                outs[0][place % batch] = row.astype(jnp.bfloat16)
            else:
                outs[place][...] = row.astype(jnp.bfloat16)


def token_terms(grad, weight, side, owners, adds, parts, marks, split):
    length, width = grad.shape
    model = weight.shape[0]
    rows, pairs = length // owners, owners // 2
    batch = 2 if pairs % 2 == 0 else 1
    block = pl.BlockSpec((batch, rows, model), lambda i, side_ref: (i, 0, 0))
    single = pl.BlockSpec((rows, model), lambda i, side_ref: (0, 0))
    out_specs, out_shape = block, jax.ShapeDtypeStruct((pairs, rows, model), jnp.bfloat16)
    if split:
        out_specs = (single,) * pairs
        out_shape = (jax.ShapeDtypeStruct((rows, model), jnp.bfloat16),) * pairs
    return pl.pallas_call(
        functools.partial(token_kernel, len(adds), len(parts), len(marks)),
        grid_spec=pltpu.PrefetchScalarGridSpec(
            num_scalar_prefetch=1,
            grid=(pairs // batch,),
            in_specs=[
                pl.BlockSpec(
                    (batch, None, rows, width), lambda i, side_ref: (i, side_ref[0], 0, 0)
                ),
                pl.BlockSpec((model, width), lambda i, side_ref: (0, 0)),
            ]
            + [block] * len(adds)
            + [single] * len(parts)
            + [pl.BlockSpec(memory_space=pltpu.HBM)] * len(marks),
            out_specs=out_specs,
        ),
        out_shape=out_shape,
        compiler_params=pltpu.CompilerParams(vmem_limit_bytes=65024 * 1024),
        cost_estimate=pl.CostEstimate(
            flops=length * width, bytes_accessed=length * width, transcendentals=0
        ),
        name="token_terms",
    )(side.reshape(1), grad.reshape(pairs, 2, rows, width), weight, *adds, *parts, *marks)


def mix_kernel(outs, count, marks, *refs):
    sources, refs = refs[:count], refs[count + marks :]
    targets, extra, sem = refs[: len(outs)], refs[len(outs) : -1], refs[-1]
    mine = lax.axis_index("dp")

    def each(act):
        for index, cases in enumerate(outs):
            for low, high, terms in cases:
                copies = []

                @pl.when((mine >= low) & (mine < high))
                def _():
                    for slot, (source, place) in enumerate(terms):
                        ref = sources[source]
                        ref = ref if place is None else ref.at[mine + place]
                        target = targets[index] if slot == 0 else extra[index]
                        copies.append(pltpu.make_async_copy(ref, target, sem.at[index, slot]))
                    act(index, copies)

    def start(index, copies):
        for copy in copies:
            copy.start()

    def finish(index, copies):
        for copy in copies:
            copy.wait()
        if len(copies) > 1:
            total = targets[index][...].astype(jnp.float32) + extra[index][...].astype(jnp.float32)
            targets[index][...] = total.astype(jnp.bfloat16)

    each(start)
    each(finish)


def mix(outs, sources, marks):
    shape = sources[0].shape[-2:]
    plain = pl.BlockSpec(memory_space=pl.ANY)
    vmem = pl.BlockSpec(memory_space=pltpu.VMEM)
    return pl.pallas_call(
        functools.partial(mix_kernel, outs, len(sources), len(marks)),
        out_shape=(jax.ShapeDtypeStruct(shape, jnp.bfloat16),) * len(outs),
        in_specs=[plain] * (len(sources) + len(marks)),
        out_specs=(vmem,) * len(outs),
        scratch_shapes=[pltpu.VMEM(shape, jnp.bfloat16)] * len(outs)
        + [pltpu.SemaphoreType.DMA((len(outs), 2))],
        compiler_params=pltpu.CompilerParams(vmem_limit_bytes=65024 * 1024),
        cost_estimate=pl.CostEstimate(flops=1, bytes_accessed=1, transcendentals=0),
        name="mix",
    )(*sources, *marks)


def scatter_cases(planes, step, terms, received_up, received_down):
    first, last = planes - step, step - planes
    ups = [(0, 1, [(terms, first)]), (1, step, [(terms, first), (received_up, None)])]
    downs = [
        (planes - 1, planes, [(terms, last)]),
        (planes - step, planes - 1, [(terms, last), (received_down, None)]),
    ]
    return ups, downs


def total_kernel(share, layout, count, *refs):
    sources, outs, pieces, sem = refs[:count], refs[count : count + 3], refs[count + 3 : -1], refs[-1]
    mine = lax.axis_index("dp")

    def each(act):
        for index, cases in enumerate(layout):
            for low, high, source, own in cases:

                @pl.when((mine >= low) & (mine < high))
                def _():
                    ref = sources[source].at[mine] if own else sources[source]
                    act(pltpu.make_async_copy(ref, pieces[index], sem.at[index]))

    each(lambda copy: copy.start())
    each(lambda copy: copy.wait())
    wide = share * HEAD_WIDTH
    for group in range(len(layout) // 3):
        total = sum(pieces[3 * group + index][...].astype(jnp.float32) for index in range(3))
        outs[0][:, group * wide : (group + 1) * wide] = total[:, :wide]
        narrow = slice(group * HEAD_WIDTH, (group + 1) * HEAD_WIDTH)
        outs[1][:, narrow] = total[:, wide : wide + HEAD_WIDTH]
        outs[2][:, narrow] = total[:, wide + HEAD_WIDTH :]


def total_terms(share, layout, sources):
    groups = len(layout) // 3
    rows, width = sources[0].shape[-2:]
    plain = pl.BlockSpec(memory_space=pl.ANY)
    vmem = pl.BlockSpec(memory_space=pltpu.VMEM)
    return pl.pallas_call(
        functools.partial(total_kernel, share, layout, len(sources)),
        out_shape=tuple(
            jax.ShapeDtypeStruct((rows, groups * count * HEAD_WIDTH), jnp.float32)
            for count in (share, 1, 1)
        ),
        in_specs=[plain] * len(sources),
        out_specs=(vmem,) * 3,
        scratch_shapes=[pltpu.VMEM((rows, width), jnp.bfloat16)] * len(layout)
        + [pltpu.SemaphoreType.DMA((len(layout),))],
        compiler_params=pltpu.CompilerParams(vmem_limit_bytes=65024 * 1024),
        cost_estimate=pl.CostEstimate(flops=1, bytes_accessed=1, transcendentals=0),
        name="total_terms",
    )(*sources)


def after(value, *others):
    return lax.optimization_barrier((value, *others))[0]


def up(value, first, last):
    return lax.ppermute(value, "dp", [(i, i + 1) for i in range(first, last)])


def down(value, first, last):
    return lax.ppermute(value, "dp", [(i + 1, i) for i in range(first, last)])


def add(*terms):
    return functools.reduce(lambda a, b: a + b, [term.astype(jnp.float32) for term in terms])


def link(value, *pairs):
    return lax.ppermute(value, "dp", pairs)


ENDS = ((0, 1), (3, 2))
OUTER = ((0, 1), (1, 0), (2, 3), (3, 2))
INNER = ((1, 2), (2, 1))
OUTWARD = ((1, 0), (2, 3))


def gather_four(parts):
    outer = [link(part, *OUTER) for part in parts]
    inner = [link(part, *INNER) for part in parts]
    inner_second = [link(part, *INNER) for part in outer]
    outer_second = [link(part, *OUTWARD) for part in inner]
    outer_third = [link(part, *OUTWARD) for part in inner_second]
    own = tuple((plane, plane) for plane in range(4))
    swap = tuple((plane, plane ^ 1) for plane in range(4))
    spots = (own, swap, ((1, 2), (2, 1)), ((1, 3), (2, 0)), ((0, 2), (3, 1)), ((0, 3), (3, 0)))
    columns = zip(parts, outer, inner, inner_second, outer_second, outer_third)
    return [piece for column in columns for piece in column], spots * len(parts)


def gather_line(block, planes):
    left, right = [block], [block]
    for step in range(planes - 1):
        left.append(up(left[-1], step, planes - 1))
        right.append(down(right[-1], 0, planes - 1 - step))
    spots = [tuple((plane, plane - hop) for plane in range(hop, planes)) for hop in range(planes)]
    spots += [
        tuple((plane, plane + hop) for plane in range(planes - hop)) for hop in range(1, planes)
    ]
    return left + right[1:], tuple(spots)


def stacked(terms, planes):
    return terms.reshape(planes, terms.shape[0] // planes, terms.shape[1])


def scatter_step(planes, step, terms, received, marks=()):
    ups, downs = scatter_cases(planes, step, 0, 1, 2)
    if step == 1:
        ups, downs = ups[:1], downs[:1]
    left, right = mix((ups, downs), (terms, *received), marks)
    received = up(left, 0, step), down(right, planes - 1 - step, planes - 1)
    return received, (left, right)


def exchange_cases(step, terms, outer, inner):
    place = 4 - step
    ends = [(0, 1, [(terms, place)]), (3, 4, [(terms, -place)])]
    if step == 1:
        return ends, []
    inward = [(1, 2, [(terms, place), (outer, None)]), (2, 3, [(terms, -place), (outer, None)])]
    outward = [(1, 2, [(terms, -place), (inner, None)]), (2, 3, [(terms, place), (inner, None)])]
    return ends + outward * (step == 3), inward


def exchange(step, terms, received, marks):
    outer, inner = mix(exchange_cases(step, 0, 1, 2), (terms, *received), marks)
    return (link(outer, *(OUTER if step == 3 else ENDS)), link(inner, *INNER)), (outer, inner)


def whole(planes, first):
    return [
        [(0, planes, first, True)],
        [(0, planes, first + 1, False)],
        [(0, planes, first + 2, False)],
    ]


def local(planes, owners, tokens, q_weight, key_projection, value_projection, q_gain, k_gain, doc_lengths, out_cot):
    groups = key_projection.shape[1] // HEAD_WIDTH
    share = q_weight.shape[1] // key_projection.shape[1]
    wide = share * HEAD_WIDTH
    row_tokens = lax.all_gather(tokens, "seq", axis=0, tiled=True)
    length, model = row_tokens.shape
    rows = length // owners
    tables = doc_tables(doc_lengths[0], length)
    gains = (q_gain[None, :], k_gain[None, :])
    me = lax.axis_index("seq")
    side, pair = lax.rem(me, 2), lax.div(me, 2)

    def halves(group):
        narrow = slice(group * HEAD_WIDTH, (group + 1) * HEAD_WIDTH)
        broad = slice(group * wide, (group + 1) * wide)
        return (
            q_weight[:, broad],
            jnp.concatenate([key_projection[:, narrow], value_projection[:, narrow]], axis=1),
        )

    def group_heads(group, pieces, spots, marks=(), parts=1):
        out, grad, weight, terms = heads(
            share, parts, pieces, spots, row_tokens, tables, gains, doc_lengths,
            out_cot[:, group * wide : (group + 1) * wide], marks,
        )
        return out, grad, weight, stacked(terms, planes)

    def token_part(which, grad, weight, adds=(), parts=(), marks=(), split=False):
        return token_terms(grad, weight, which, owners, adds, parts, marks, split)

    outs, layout, sources = [], [], []
    sent = kept = ()
    paired = groups == 2 and planes == 4
    if paired:
        pieces, spots = gather_four(halves(0))
        block = after(jnp.concatenate(halves(1), axis=1), pieces[4])
        far = link(block, (0, 2), (1, 3), (2, 0), (3, 1))
        middle = link(block, *INNER)
        block = after(block, pieces[5])
        near = link(block, *OUTER)
        out, grad, weight, terms = group_heads(0, pieces, spots, parts=2)
        outs.append(out)
        (first,) = mix((exchange_cases(1, 0, None, None)[0],), (terms,), ())
        received = (link(first, *ENDS),)
        sent = (token_part(1 - side, grad, weight, marks=(first, far)),)
        last = link(far, *OUTWARD)
        outer_cases, inner_cases = exchange_cases(2, 0, 1, None)
        edges = [(0, 1, [(0, 1)]), (3, 4, [(0, -1)])]
        outer, inner, edge = mix((outer_cases, inner_cases, edges), (terms, *received), (*sent, near, middle))
        received = link(outer, *ENDS), link(inner, *INNER)
        edge_received = link(edge, *ENDS)
        old, early, marks = terms, (grad, weight), (outer, inner, edge)
        pieces = [block, near, middle, far, last]
        spots = (
            tuple((plane, plane) for plane in range(4)),
            tuple((plane, plane ^ 1) for plane in range(4)),
            ((1, 2), (2, 1)),
            tuple((plane, plane ^ 2) for plane in range(4)),
            ((0, 3), (3, 0)),
        )
        out, grad, weight, terms = group_heads(1, pieces, spots, marks)
        outs.append(out)
        outer_cases, inner_cases = exchange_cases(3, 0, 1, 2)
        outer_cases = exchange_cases(1, 3, None, None)[0] + outer_cases[2:]
        marks = mix((outer_cases, inner_cases), (old, *received, terms), (edge_received,))
        received = link(marks[0], *OUTER), link(marks[1], *INNER)
        layout = [
            [(0, 4, 0, True)],
            [(0, 4, 1, False)],
            [(0, 1, 2, False), (1, 3, 3, False), (3, 4, 2, False)],
        ]
        sources = [old, edge_received, *received]
    else:
        for group in range(groups):
            block = jnp.concatenate(halves(group), axis=1)
            out, grad, weight, terms = group_heads(group, *gather_line(block, planes))
            outs.append(out)
            received, marks = scatter_step(planes, 1, terms, ())
            if group + 1 < groups:
                for step in range(2, planes):
                    received, marks = scatter_step(planes, step, terms, received)
                layout += whole(planes, len(sources))
                sources += [terms, *received]
                sent = (token_part(1 - side, grad, weight, sent),)
                kept = (token_part(side, grad, weight, kept),)
    sent = token_part(1 - side, grad, weight, sent, marks=marks, split=True)
    swapped = [lax.ppermute(part, "seq", [(i, i ^ 1) for i in range(owners)]) for part in sent]
    forward = functools.partial(scatter_step, planes)
    if paired:
        kept = (token_part(side, *early, marks=sent),)
        forward = exchange
    received, marks = forward(2, terms, received[:1] if paired else received, kept)
    kept = token_part(side, grad, weight, kept, swapped, marks)
    shares = [lax.dynamic_index_in_dim(kept, pair, 0, keepdims=False)]
    for other in range(1, owners // 2):
        part = lax.dynamic_index_in_dim(kept, pair ^ other, 0, keepdims=False)
        shares.append(lax.ppermute(part, "seq", [(i, i ^ (2 * other)) for i in range(owners)]))
    marks = (kept,)
    for step in range(3, planes):
        received, marks = forward(step, terms, received, marks)
    spread = lax.all_to_all(
        after(jnp.concatenate(outs, axis=1), *marks),
        "seq",
        split_axis=0,
        concat_axis=0,
        tiled=True,
    )
    layout += whole(planes, len(sources))
    sources += [terms, *received]
    attn_out = spread.reshape(owners, rows, groups * wide).transpose(1, 0, 2)
    attn_out = attn_out.reshape(rows, owners * groups * wide)
    sources[0] = after(sources[0], attn_out)
    weight_grads = total_terms(share, layout, sources)
    token_grad = add(*shares).astype(jnp.bfloat16)
    return (attn_out, token_grad, *weight_grads)


def solution(mesh):
    rows, split = P(("dp", "seq"), None), P("dp", "seq")
    return jax.shard_map(
        functools.partial(local, mesh.shape["dp"], mesh.shape["seq"]),
        mesh=mesh,
        in_specs=(rows, split, split, split, P(), P(), P("dp", None), split),
        out_specs=(rows, rows, split, split, split),
        check_vma=False,
    )
```
